32 devices in a mesh: energy: 8 (over z, y), col: 4 (over x, core).
Axes of the slice: x: 2, y: 2, z: 4, core: 2. Of those that a mesh axis runs over, the one named last changes fastest.
Arguments:
- lesser: float32 [128, 2, 12, 1152], P('energy', None, 'col'), may hold values from -6 to 6
- greater_transposed: float32 [128, 2, 12, 1152], P('energy', None, 'col'), may hold values from -6 to 6
- coulomb: bfloat16 [1152, 1152], P('energy', 'col'), may hold values from -0.1875 to 0.1875
Outputs:
- screened: float32 [128, 2, 12, 1152], P('energy', None, 'col')
The draws below stay inside these ranges and needn't reach their ends.
All inputs are finite; a program needn't handle non-finite values.
Results may differ from the reference program's by a relative error of at most 0.0029.
Values may be sent and summed in bfloat16 or wider, within the bound.
A program may use at most 64 MiB of HBM per device.

```python
import math
import jax
import jax.numpy as jnp

NB = 1152
ENERGIES = 128
COLS = 12


def block_levels(own_key, extent, split, low, high):
    def one(position, shards_of):
        steps = jax.random.uniform(jax.random.fold_in(jax.random.fold_in(own_key, 6), position), (shards_of,), jnp.float32, low / len(split), high / len(split))
        return jnp.repeat(jnp.exp(steps), extent[position] // shards_of).reshape((-1,) + (1,) * (len(extent) - position - 1))

    gain = one(*split[0])
    for cut in split[1:]:
        gain = gain * one(*cut)
    return gain


def noise(stream_key, extent, width, limit, pieces=(), dtype=jnp.bfloat16):
    gain = block_levels(stream_key, extent, pieces, -0.22, 0.18) if pieces else 1.0
    result = jax.random.normal(stream_key, extent, jnp.float32) * width * gain
    return jnp.minimum(jnp.maximum(result, -limit), limit).astype(dtype)


def setup_inputs(seed: int = 0) -> dict:
    keys = jax.random.split(jax.random.key(seed), 4)
    lesser = noise(keys[0], (ENERGIES, 2, COLS, NB), 1.0, 6.0, ((0, 8), (2, 4)), jnp.float32)
    greater_transposed = noise(keys[1], (ENERGIES, 2, COLS, NB), 1.0, 6.0, ((0, 8), (2, 4)), jnp.float32)
    coulomb = noise(keys[2], (NB, NB), NB ** -0.5, 0.1875, ((0, 8), (1, 4)))
    return {"lesser": lesser, "greater_transposed": greater_transposed, "coulomb": coulomb}


def reference(lesser, greater_transposed, coulomb):
    energies = lesser.shape[0]
    padded = 2 * energies
    left = lesser[:, 0] + 1j * lesser[:, 1]
    right = greater_transposed[:, 0] + 1j * greater_transposed[:, 1]
    left_hat = jnp.fft.fft(left, n=padded, axis=0)
    right_pad = jnp.pad(right, ((0, energies), (0, 0), (0, 0)))
    right_flip = jnp.roll(jnp.flip(right_pad, 0), 1, axis=0)
    corr = jnp.fft.ifft(left_hat * jnp.fft.fft(right_flip, axis=0), axis=0)[:energies]
    factor = 1.0 / math.sqrt(energies)
    polarized = jnp.stack([corr.imag * factor, -corr.real * factor], axis=1).astype(jnp.bfloat16)
    flattened = polarized.reshape(-1, coulomb.shape[0])
    screened = jnp.dot(flattened, coulomb, preferred_element_type=jnp.float32)
    return screened.reshape(lesser.shape)
```

```python
import functools
import math

import jax
import jax.numpy as jnp
import ml_dtypes
import numpy as np
from jax import lax
from jax.experimental import pallas as pl
from jax.experimental.pallas import tpu as pltpu
from jax.sharding import PartitionSpec as P

LANES = 128
REST = 32
MESH = pl.DeviceIdType.MESH


def product(left, right):
    return jnp.dot(left, right, precision=lax.Precision.HIGHEST, preferred_element_type=jnp.float32)


def per_device(lesser, greater_transposed, coulomb):
    lesser_all, greater_all = (
        lax.all_to_all(lesser, "energy", split_axis=3, concat_axis=0, tiled=True),
        lax.all_to_all(greater_transposed, "energy", split_axis=3, concat_axis=0, tiled=True),
    )
    energies = lesser_all.shape[0]
    columns_here = lesser_all.shape[2]
    rows_here = lesser_all.shape[3]
    padded = 2 * energies
    lesser_re = lesser_all[:, 0].reshape(energies, -1)
    lesser_im = lesser_all[:, 1].reshape(energies, -1)
    greater_re = greater_all[:, 0].reshape(energies, -1)
    greater_im = greater_all[:, 1].reshape(energies, -1)
    frequency = lax.broadcasted_iota(jnp.int32, (padded, energies), 0)
    position = lax.broadcasted_iota(jnp.int32, (padded, energies), 1)
    phases = frequency * position % padded
    angles = phases.astype(jnp.float32) * (2.0 * math.pi / padded)
    cos_table = jnp.cos(angles)
    sin_table = jnp.sin(angles)
    left_re = product(cos_table, lesser_re) + product(sin_table, lesser_im)
    left_im = product(cos_table, lesser_im) - product(sin_table, lesser_re)
    right_re = product(cos_table, greater_re) - product(sin_table, greater_im)
    right_im = product(cos_table, greater_im) + product(sin_table, greater_re)
    mixed_re = left_re * right_re - left_im * right_im
    mixed_im = left_re * right_im + left_im * right_re
    corr_re = (product(cos_table.T, mixed_re) - product(sin_table.T, mixed_im)) / padded
    corr_im = (product(cos_table.T, mixed_im) + product(sin_table.T, mixed_re)) / padded
    factor = 1.0 / math.sqrt(energies)
    polar_re = (corr_im * factor).reshape(energies, columns_here, rows_here)
    polar_im = (-corr_re * factor).reshape(energies, columns_here, rows_here)
    polarized = jnp.stack([polar_re, polar_im], axis=1).astype(jnp.bfloat16)
    coulomb_wide = lax.all_gather(coulomb, "col", axis=1, tiled=True)
    order = coulomb_wide.shape[1]
    returned = lax.all_to_all(polarized, "energy", split_axis=0, concat_axis=3, tiled=True)
    flattened = returned.reshape(-1, order)
    running = jnp.dot(
        flattened,
        lax.all_gather(coulomb_wide, "energy", axis=0, tiled=True),
        preferred_element_type=jnp.float32,
    )
    screened = running.reshape(returned.shape)
    return screened


def split_table(table):
    high = table.astype(ml_dtypes.bfloat16)
    low = (table - high.astype(np.float64)).astype(ml_dtypes.bfloat16)
    return np.concatenate([high, high, low], axis=1)


def tables(energies):
    padded = 2 * energies
    angle = 2.0 * math.pi / padded * (np.outer(np.arange(padded), np.arange(energies)) % padded)
    cos, sin = np.cos(angle), np.sin(angle)
    forward_re = np.stack([cos, sin], axis=2).reshape(padded, padded)
    forward_im = np.stack([-sin, cos], axis=2).reshape(padded, padded)
    forward = np.concatenate([forward_re, forward_im], axis=0)
    scale = 1.0 / (padded * math.sqrt(energies))
    corr_re = np.concatenate([cos.T, -sin.T], axis=1)
    corr_im = np.concatenate([sin.T, cos.T], axis=1)
    inverse = np.stack([corr_im, -corr_re], axis=1).reshape(padded, 2 * padded) * scale
    return split_table(forward), split_table(inverse)


def high_low(x):
    high = x.astype(jnp.bfloat16)
    return high, (x - high.astype(jnp.float32)).astype(jnp.bfloat16)


def kernel(n, m, l_ref, r_ref, w_ref, tf_ref, ti_ref, o_ref, give, take, polar, panel, coul,
           lr_send, lr_recv, p_send, p_recv, c_send, c_recv, own_sem):
    here_e, here_c = lax.axis_index("energy"), lax.axis_index("col")
    block, cols, _, order = l_ref.shape
    tiles_k = order // LANES
    total = cols * tiles_k
    full, extra = total // n, total % n
    slots = full + (1 if extra else 0)
    rows = 2 * block
    depth, width = w_ref.shape
    wide = width - REST
    groups = LANES // REST
    third = depth // 3

    z, y = here_e // 2, lax.rem(here_e, 2)
    x, core = here_c // 2, lax.rem(here_c, 2)
    nz = n // 2

    def at_e(s, b):
        return lax.rem(z + nz - s, nz) * 2 + (y if b == 0 else 1 - y)

    def at_c(a):
        return (x if a == 0 else 1 - x) * 2 + core

    peer_y = z * 2 + 1 - y
    peer_x = (1 - x) * 2 + core
    peer_core = x * 2 + 1 - core

    barrier = pltpu.get_barrier_semaphore()
    for s in range(1, n):
        pl.semaphore_signal(barrier, inc=1, device_id={"energy": lax.rem(here_e + s, n)}, device_id_type=MESH)
    for peer in (peer_x, peer_core):
        pl.semaphore_signal(barrier, inc=1, device_id={"col": peer}, device_id_type=MESH)

    sign = jnp.where(lax.broadcasted_iota(jnp.int32, (rows, LANES), 0) % 2 == 0, 1.0, -1.0)
    for t in range(slots * n):
        j, d = t // n, t % n
        if t >= total:
            continue
        c, k = t // tiles_k, t % tiles_k
        lanes = slice(k * LANES, (k + 1) * LANES)
        high, low = high_low(l_ref[:, c, :, lanes].reshape(rows, LANES))
        give[d, j, 0:rows] = high
        give[d, j, rows:2 * rows] = low
        right = r_ref[:, c, :, lanes].reshape(rows, LANES) * sign
        give[d, j, 2 * rows:3 * rows] = right.astype(jnp.bfloat16)

    pl.semaphore_wait(barrier, n - 1 + 2)

    sends = []

    def parts(source, target, sems_s, sems_r, s, dev, has_extra):
        if full:
            cp = pltpu.make_async_remote_copy(
                src_ref=source(0, full), dst_ref=target(0, full), send_sem=sems_s.at[0, s],
                recv_sem=sems_r.at[0, s], device_id={"energy": dev}, device_id_type=MESH)
            cp.start()
            sends.append((cp, None))
        if extra:
            cq = pltpu.make_async_remote_copy(
                src_ref=source(full, 1), dst_ref=target(full, 1), send_sem=sems_s.at[1, s],
                recv_sem=sems_r.at[1, s], device_id={"energy": dev}, device_id_type=MESH)
            pl.when(has_extra)(cq.start)
            sends.append((cq, has_extra))

    for s in range(1, n):
        dev = lax.rem(here_e + s, n)
        parts(lambda a, w: give.at[dev, pl.ds(a, w)], lambda a, w: take.at[pl.ds(a, w), here_e],
              lr_send, lr_recv, s, dev, dev < extra)
    own = pltpu.make_async_copy(give.at[here_e], take.at[:, here_e], own_sem.at[0])
    own.start()

    w = w_ref[...]
    coul[here_e, here_c, 0:depth] = w[:, 0:LANES]
    coul[here_e, here_c, depth:2 * depth] = w[:, LANES:2 * LANES]
    rest = w[:, wide:].astype(jnp.float32)
    packed = jnp.concatenate(
        [rest[q * third:(q + 1) * third] for q in range(3)] + [jnp.zeros((third, LANES - 3 * REST), jnp.float32)],
        axis=1)
    coul[here_e, here_c, 2 * depth:2 * depth + third] = packed.astype(jnp.bfloat16)

    got = {}

    def share(index, e, c, dev):
        cp = pltpu.make_async_remote_copy(
            src_ref=coul.at[e, c], dst_ref=coul.at[e, c], send_sem=c_send.at[index],
            recv_sem=c_recv.at[index], device_id=dev, device_id_type=MESH)
        cp.start()
        sends.append((cp, None))
        got[index] = cp

    iz, iy, ix, ic = 0, nz, 2 * nz, 4 * nz
    for s in range(1, nz):
        share(iz + s, here_e, here_c, {"energy": lax.rem(z + s, nz) * 2 + y})
    share(iy, here_e, here_c, {"energy": peer_y})
    share(ix, here_e, here_c, {"col": peer_x})
    share(ic, here_e, here_c, {"col": peer_core})
    for s in range(1, nz):
        got[iz + s].wait_recv()
        e = at_e(s, 0)
        share(iy + s, e, here_c, {"energy": peer_y})
        share(ix + 2 * s, e, here_c, {"col": peer_x})
        share(ic + 4 * s, e, here_c, {"col": peer_core})
    for s in range(nz):
        got[iy + s].wait_recv()
        e = at_e(s, 1)
        share(ix + 2 * s + 1, e, here_c, {"col": peer_x})
        share(ic + 4 * s + 2, e, here_c, {"col": peer_core})

    def arrive(source, target, sems_s, sems_r, s):
        dev = lax.rem(here_e + s, n)
        if full:
            pltpu.make_async_remote_copy(
                src_ref=source(0, full), dst_ref=target(0, full), send_sem=sems_s.at[0, s],
                recv_sem=sems_r.at[0, s], device_id={"energy": dev}, device_id_type=MESH).wait_recv()

    def arrive_extra(source, target, sems_s, sems_r, s, has):
        dev = lax.rem(here_e + s, n)
        if extra:
            pl.when(has)(pltpu.make_async_remote_copy(
                src_ref=source(full, 1), dst_ref=target(full, 1), send_sem=sems_s.at[1, s],
                recv_sem=sems_r.at[1, s], device_id={"energy": dev}, device_id_type=MESH).wait_recv)

    own.wait()
    for s in range(1, n):
        src, dst = (lambda a, w: give.at[0, pl.ds(a, w)]), (lambda a, w: take.at[pl.ds(a, w), 0])
        arrive(src, dst, lr_send, lr_recv, s)
        arrive_extra(src, dst, lr_send, lr_recv, s, here_e < extra)

    def piece(i):
        return jnp.concatenate(
            [take[j, :, i * rows:(i + 1) * rows].reshape(n * rows, LANES) for j in range(slots)], axis=1)

    l_high, l_low, r_high = piece(0), piece(1), piece(2)
    span = n * rows
    left = jnp.dot(tf_ref[...], jnp.concatenate([l_high, l_low, l_high], axis=0),
                   preferred_element_type=jnp.float32)
    right = jnp.dot(tf_ref[:, span:], jnp.concatenate([r_high, r_high], axis=0),
                    preferred_element_type=jnp.float32)
    a, b = left[:span], left[span:]
    c, d = right[:span], right[span:]
    mixed = jnp.concatenate([a * c + b * d, b * c - a * d], axis=0)
    m_high, m_low = high_low(mixed)
    polarized = jnp.dot(ti_ref[...], jnp.concatenate([m_high, m_low, m_high], axis=0),
                        preferred_element_type=jnp.float32).astype(jnp.bfloat16)
    for j in range(slots):
        polar[j] = polarized[:, j * LANES:(j + 1) * LANES].reshape(n, rows, LANES)

    for s in range(1, n):
        dev = lax.rem(here_e + s, n)
        parts(lambda a, w: polar.at[pl.ds(a, w), dev], lambda a, w: panel.at[pl.ds(a, w), here_e],
              p_send, p_recv, s, dev, here_e < extra)
    own_p = pltpu.make_async_copy(polar.at[:, here_e], panel.at[:, here_e], own_sem.at[1])
    own_p.start()

    for s in range(nz):
        for b in range(2):
            got[ix + 2 * s + b].wait_recv()
            share(ic + 4 * s + 2 * b + 1, at_e(s, b), at_c(1), {"col": peer_core})
    for i in range(4 * nz):
        got[ic + i].wait_recv()

    lane = lax.broadcasted_iota(jnp.int32, (third, LANES), 1)
    rests = []
    for g in range(n):
        for q in range(3):
            acc = jnp.zeros((third, LANES), jnp.float32)
            for cc in range(m):
                u = coul[g, cc, 2 * depth:2 * depth + third].astype(jnp.float32)
                shift = (cc - q) * REST % LANES
                if shift:
                    u = pltpu.roll(u, shift, 1)
                acc = jnp.where((lane >= cc * REST) & (lane < (cc + 1) * REST), u, acc)
            rests.append(acc.astype(jnp.bfloat16))
    rest_all = jnp.concatenate(rests, axis=0)

    own_p.wait()
    for s in range(1, n):
        src, dst = (lambda a, w: polar.at[pl.ds(a, w), 0]), (lambda a, w: panel.at[pl.ds(a, w), 0])
        arrive(src, dst, p_send, p_recv, s)
        arrive_extra(src, dst, p_send, p_recv, s, lax.rem(here_e + n - s, n) < extra)

    flat = jnp.concatenate(
        [jnp.concatenate([panel[t // n, t % n] for t in range(c * tiles_k, (c + 1) * tiles_k)], axis=1)
         for c in range(cols)], axis=0)
    rest_out = jnp.dot(flat, rest_all, preferred_element_type=jnp.float32)
    pieces = []
    for cc in range(m):
        weight = jnp.concatenate(
            [coul[:, cc, h * depth:(h + 1) * depth].reshape(n * depth, LANES) for h in range(2)], axis=1)
        pieces.append(jnp.dot(flat, weight, preferred_element_type=jnp.float32))
        pieces.append(rest_out[:, cc * REST:(cc + 1) * REST])
    o_ref[...] = jnp.concatenate(pieces, axis=1)

    for cp, cond in sends:
        if cond is None:
            cp.wait_send()
        else:
            pl.when(cond)(cp.wait_send)


def fused(n, m, lesser, greater_transposed, coulomb):
    block, _, cols, order = lesser.shape
    depth, width = coulomb.shape
    energies = n * block
    total = cols * order // LANES
    slots = -(-total // n)
    rows = 2 * block
    forward, inverse = tables(energies)
    vmem = pl.BlockSpec(memory_space=pltpu.VMEM)
    out = pl.pallas_call(
        functools.partial(kernel, n, m),
        out_shape=jax.ShapeDtypeStruct((cols * rows, order), jnp.float32),
        in_specs=[vmem] * 5,
        out_specs=vmem,
        scratch_shapes=[
            pltpu.VMEM((n, slots, 3 * rows, LANES), jnp.bfloat16),
            pltpu.VMEM((slots, n, 3 * rows, LANES), jnp.bfloat16),
            pltpu.VMEM((slots, n, rows, LANES), jnp.bfloat16),
            pltpu.VMEM((slots, n, rows, LANES), jnp.bfloat16),
            pltpu.VMEM((n, m, 2 * depth + depth // 3, LANES), jnp.bfloat16),
            pltpu.SemaphoreType.DMA((2, n)),
            pltpu.SemaphoreType.DMA((2, n)),
            pltpu.SemaphoreType.DMA((2, n)),
            pltpu.SemaphoreType.DMA((2, n)),
            pltpu.SemaphoreType.DMA((n * m,)),
            pltpu.SemaphoreType.DMA((n * m,)),
            pltpu.SemaphoreType.DMA((2,)),
        ],
        compiler_params=pltpu.CompilerParams(
            collective_id=0, has_side_effects=True, vmem_limit_bytes=40 * 2**20),
        cost_estimate=pl.CostEstimate(flops=2_000_000_000, bytes_accessed=8_000_000, transcendentals=0),
    )(lesser.transpose(0, 2, 1, 3), greater_transposed.transpose(0, 2, 1, 3), coulomb,
      jnp.asarray(forward), jnp.asarray(inverse))
    return out.reshape(cols, block, 2, order).transpose(1, 2, 0, 3)


def solution(mesh):
    placed = (P("energy", None, "col", None), P("energy", None, "col", None), P("energy", "col"))
    n, m = mesh.shape["energy"], mesh.shape["col"]

    def local(lesser, greater_transposed, coulomb):
        depth, width = coulomb.shape
        fits = (m == 4 and n % 2 == 0 and depth % 48 == 0 and width == 2 * LANES + REST
                and lesser.shape[0] % 8 == 0 and lesser.shape[3] % LANES == 0)
        if fits:
            return fused(n, m, lesser, greater_transposed, coulomb)
        return per_device(lesser, greater_transposed, coulomb)

    return jax.shard_map(
        local,
        mesh=mesh,
        in_specs=placed,
        out_specs=P("energy", None, "col", None),
        check_vma=False,
    )
```

```python
import functools
import math

import jax
import jax.numpy as jnp
import ml_dtypes
import numpy as np
from jax import lax
from jax.experimental import pallas as pl
from jax.experimental.pallas import tpu as pltpu
from jax.sharding import PartitionSpec as P

LANES = 128
REST = 32
MESH = pl.DeviceIdType.MESH


def product(left, right):
    return jnp.dot(left, right, precision=lax.Precision.HIGHEST, preferred_element_type=jnp.float32)


def per_device(lesser, greater_transposed, coulomb):
    lesser_all, greater_all = (
        lax.all_to_all(lesser, "energy", split_axis=3, concat_axis=0, tiled=True),
        lax.all_to_all(greater_transposed, "energy", split_axis=3, concat_axis=0, tiled=True),
    )
    energies = lesser_all.shape[0]
    columns_here = lesser_all.shape[2]
    rows_here = lesser_all.shape[3]
    padded = 2 * energies
    lesser_re = lesser_all[:, 0].reshape(energies, -1)
    lesser_im = lesser_all[:, 1].reshape(energies, -1)
    greater_re = greater_all[:, 0].reshape(energies, -1)
    greater_im = greater_all[:, 1].reshape(energies, -1)
    frequency = lax.broadcasted_iota(jnp.int32, (padded, energies), 0)
    position = lax.broadcasted_iota(jnp.int32, (padded, energies), 1)
    phases = frequency * position % padded
    angles = phases.astype(jnp.float32) * (2.0 * math.pi / padded)
    cos_table = jnp.cos(angles)
    sin_table = jnp.sin(angles)
    left_re = product(cos_table, lesser_re) + product(sin_table, lesser_im)
    left_im = product(cos_table, lesser_im) - product(sin_table, lesser_re)
    right_re = product(cos_table, greater_re) - product(sin_table, greater_im)
    right_im = product(cos_table, greater_im) + product(sin_table, greater_re)
    mixed_re = left_re * right_re - left_im * right_im
    mixed_im = left_re * right_im + left_im * right_re
    corr_re = (product(cos_table.T, mixed_re) - product(sin_table.T, mixed_im)) / padded
    corr_im = (product(cos_table.T, mixed_im) + product(sin_table.T, mixed_re)) / padded
    factor = 1.0 / math.sqrt(energies)
    polar_re = (corr_im * factor).reshape(energies, columns_here, rows_here)
    polar_im = (-corr_re * factor).reshape(energies, columns_here, rows_here)
    polarized = jnp.stack([polar_re, polar_im], axis=1).astype(jnp.bfloat16)
    coulomb_wide = lax.all_gather(coulomb, "col", axis=1, tiled=True)
    order = coulomb_wide.shape[1]
    returned = lax.all_to_all(polarized, "energy", split_axis=0, concat_axis=3, tiled=True)
    flattened = returned.reshape(-1, order)
    running = jnp.dot(
        flattened,
        lax.all_gather(coulomb_wide, "energy", axis=0, tiled=True),
        preferred_element_type=jnp.float32,
    )
    screened = running.reshape(returned.shape)
    return screened


def split_table(table):
    high = table.astype(ml_dtypes.bfloat16)
    low = (table - high.astype(np.float64)).astype(ml_dtypes.bfloat16)
    return np.concatenate([high, high, low], axis=1)


def tables(energies):
    padded = 2 * energies
    angle = 2.0 * math.pi / padded * (np.outer(np.arange(padded), np.arange(energies)) % padded)
    cos, sin = np.cos(angle), np.sin(angle)
    forward_re = np.stack([cos, sin], axis=2).reshape(padded, padded)
    forward_im = np.stack([-sin, cos], axis=2).reshape(padded, padded)
    forward = np.concatenate([forward_re, forward_im], axis=0)
    scale = 1.0 / (padded * math.sqrt(energies))
    corr_re = np.concatenate([cos.T, -sin.T], axis=1)
    corr_im = np.concatenate([sin.T, cos.T], axis=1)
    inverse = np.stack([corr_im, -corr_re], axis=1).reshape(padded, 2 * padded) * scale
    return split_table(forward), split_table(inverse)


def high_low(x):
    high = x.astype(jnp.bfloat16)
    return high, (x - high.astype(jnp.float32)).astype(jnp.bfloat16)


def kernel(n, m, l_hbm, r_hbm, w_hbm, tf_hbm, ti_hbm, o_ref, l_ref, r_ref, w_ref, tf_ref, ti_ref,
           give, take, polar, panel, coul, lr_send, lr_recv, p_send, p_recv, c_send, c_recv, own_sem, load_sem):
    here_e, here_c = lax.axis_index("energy"), lax.axis_index("col")
    block, cols, _, order = l_ref.shape
    tiles_k = order // LANES
    total = cols * tiles_k
    full, extra = total // n, total % n
    slots = full + (1 if extra else 0)
    rows = 2 * block
    depth, width = w_ref.shape
    wide = width - REST
    third = depth // 3
    groups = [(start, min(start + 2, slots)) for start in range(0, slots, 2)]

    loads = [pltpu.make_async_copy(a, b, load_sem.at[i]) for i, (a, b) in enumerate(
        [(l_hbm, l_ref), (r_hbm, r_ref), (w_hbm, w_ref), (tf_hbm, tf_ref), (ti_hbm, ti_ref)])]
    for load in loads:
        load.start()

    z, y = here_e // 2, lax.rem(here_e, 2)
    x, core = here_c // 2, lax.rem(here_c, 2)
    nz = n // 2
    peer_y = z * 2 + 1 - y
    peer_x = (1 - x) * 2 + core
    peer_core = x * 2 + 1 - core

    barrier = pltpu.get_barrier_semaphore()
    for s in range(1, n):
        pl.semaphore_signal(barrier, inc=1, device_id={"energy": lax.rem(here_e + s, n)}, device_id_type=MESH)
    for peer in (peer_x, peer_core):
        pl.semaphore_signal(barrier, inc=1, device_id={"col": peer}, device_id_type=MESH)

    sign = jnp.where(lax.broadcasted_iota(jnp.int32, (rows, LANES), 0) % 2 == 0, 1.0, -1.0)

    def pack(t):
        j, d = t // n, t % n
        c, k = t // tiles_k, t % tiles_k
        lanes = slice(k * LANES, (k + 1) * LANES)
        high, low = high_low(l_ref[:, c, :, lanes].reshape(rows, LANES))
        give[d, j, 0:rows] = high
        give[d, j, rows:2 * rows] = low
        right = r_ref[:, c, :, lanes].reshape(rows, LANES) * sign
        give[d, j, 2 * rows:3 * rows] = right.astype(jnp.bfloat16)

    def exchange(source, target, send_sems, recv_sems, send_if, recv_if):
        out = []
        for i, (start, stop) in enumerate(groups):
            copies = []
            for s in range(1, n):
                dev = lax.rem(here_e + s, n)
                whole = min(stop, full) - start
                if whole:
                    copies.append((pltpu.make_async_remote_copy(
                        src_ref=source(start, whole, dev), dst_ref=target(start, whole),
                        send_sem=send_sems.at[2 * i, s], recv_sem=recv_sems.at[2 * i, s],
                        device_id={"energy": dev}, device_id_type=MESH), None, None))
                if stop > full:
                    copies.append((pltpu.make_async_remote_copy(
                        src_ref=source(full, 1, dev), dst_ref=target(full, 1),
                        send_sem=send_sems.at[2 * i + 1, s], recv_sem=recv_sems.at[2 * i + 1, s],
                        device_id={"energy": dev}, device_id_type=MESH), send_if(s), recv_if(s)))
            out.append(copies)
        return out

    def when(cond, f):
        if cond is None:
            f()
        else:
            pl.when(cond)(f)

    panels = exchange(
        lambda a, w, dev: give.at[dev, pl.ds(a, w)], lambda a, w: take.at[pl.ds(a, w), here_e],
        lr_send, lr_recv, lambda s: lax.rem(here_e + s, n) < extra, lambda s: here_e < extra)
    back = exchange(
        lambda a, w, dev: polar.at[pl.ds(a, w), dev], lambda a, w: panel.at[pl.ds(a, w), here_e],
        p_send, p_recv, lambda s: here_e < extra, lambda s: lax.rem(here_e + n - s, n) < extra)

    places = [(0, 0)] + [(way, s) for s in range(1, nz) for way in (1, -1)]

    def share(index, e, c, dev):
        return pltpu.make_async_remote_copy(
            src_ref=coul.at[e, c], dst_ref=coul.at[e, c], send_sem=c_send.at[index],
            recv_sem=c_recv.at[index], device_id=dev, device_id_type=MESH)

    def inside(position):
        return (position >= 0) & (position < nz)

    count = len(places)
    iz, iy, ix, ic = 0, count, 2 * count, 4 * count
    held, line, line_if, over_y, over_x, over_core = {}, {}, {}, {}, {}, {}
    for k, (way, s) in enumerate(places):
        zk = lax.rem(z - way * s + nz, nz)
        held[k] = None if k == 0 else inside(z - way * s)
        owner = (zk * 2 + y, zk * 2 + 1 - y)
        over_y[k] = share(iy + k, owner[0], here_c, {"energy": peer_y})
        for b in range(2):
            over_x[k, b] = share(ix + 2 * k + b, owner[b], here_c, {"col": peer_x})
            for a in range(2):
                over_core[k, b, a] = share(
                    ic + 4 * k + 2 * b + a, owner[b], here_c if a == 0 else peer_x, {"col": peer_core})
        if k:
            before = lax.rem(z - way * (s - 1) + nz, nz)
            line[k] = share(iz + k, before * 2 + y, here_c, {"energy": lax.rem(z + way + nz, nz) * 2 + y})
            line_if[k] = inside(z - way * (s - 1)) & inside(z + way)

    loads[0].wait()
    loads[1].wait()
    first = groups[0][1] * n
    for t in range(min(first, total)):
        pack(t)
    pl.semaphore_wait(barrier, n - 1 + 2)
    for cp, cond, _ in panels[0]:
        when(cond, cp.start)

    loads[2].wait()
    w = w_ref[...]
    coul[here_e, here_c, 0:depth] = w[:, 0:LANES]
    coul[here_e, here_c, depth:2 * depth] = w[:, LANES:2 * LANES]
    rest = w[:, wide:].astype(jnp.float32)
    packed = jnp.concatenate(
        [rest[q * third:(q + 1) * third] for q in range(3)] + [jnp.zeros((third, LANES - 3 * REST), jnp.float32)],
        axis=1)
    coul[here_e, here_c, 2 * depth:2 * depth + third] = packed.astype(jnp.bfloat16)
    for k, (way, s) in enumerate(places):
        if s == 1:
            when(line_if[k], line[k].start)
    over_y[0].start()
    over_x[0, 0].start()
    over_core[0, 0, 0].start()

    for t in range(first, total):
        pack(t)
    for copies in panels[1:]:
        for cp, cond, _ in copies:
            when(cond, cp.start)
    own = pltpu.make_async_copy(give.at[here_e], take.at[:, here_e], own_sem.at[0])
    own.start()

    def relay():
        for k, (way, s) in enumerate(places):
            if k == 0:
                continue

            def pass_on(k=k, s=s, way=way):
                line[k].wait_recv()
                if s + 1 < nz:
                    after = places.index((way, s + 1))
                    pl.when(line_if[after])(line[after].start)
                over_y[k].start()
                over_x[k, 0].start()
                over_core[k, 0, 0].start()

            when(held[k], pass_on)
        for k in range(count):

            def pass_y(k=k):
                over_y[k].wait_recv()
                over_x[k, 1].start()
                over_core[k, 1, 0].start()

            when(held[k], pass_y)

    span = n * rows

    def correlate(i):
        start, stop = groups[i]
        for cp, _, cond in panels[i]:
            when(cond, cp.wait_recv)

        def piece(p):
            return jnp.concatenate(
                [take[j, :, p * rows:(p + 1) * rows].reshape(span, LANES) for j in range(start, stop)], axis=1)

        l_high, l_low, r_high = piece(0), piece(1), piece(2)
        left = jnp.dot(tf_ref[...], jnp.concatenate([l_high, l_low, l_high], axis=0),
                       preferred_element_type=jnp.float32)
        right = jnp.dot(tf_ref[:, span:], jnp.concatenate([r_high, r_high], axis=0),
                        preferred_element_type=jnp.float32)
        a, b = left[:span], left[span:]
        c, d = right[:span], right[span:]
        mixed = jnp.concatenate([a * c + b * d, b * c - a * d], axis=0)
        m_high, m_low = high_low(mixed)
        polarized = jnp.dot(ti_ref[...], jnp.concatenate([m_high, m_low, m_high], axis=0),
                            preferred_element_type=jnp.float32).astype(jnp.bfloat16)
        for j in range(start, stop):
            polar[j] = polarized[:, (j - start) * LANES:(j - start + 1) * LANES].reshape(n, rows, LANES)
        for cp, cond, _ in back[i]:
            when(cond, cp.start)

    loads[3].wait()
    loads[4].wait()
    own.wait()
    for i in range(len(groups)):
        correlate(i)
        if i == 0:
            relay()
    own_p = pltpu.make_async_copy(polar.at[:, here_e], panel.at[:, here_e], own_sem.at[1])
    own_p.start()

    for k in range(count):

        def pass_x(k=k):
            for b in range(2):
                over_x[k, b].wait_recv()
                over_core[k, b, 1].start()

        when(held[k], pass_x)
    for k in range(count):

        def arrive(k=k):
            for b in range(2):
                for a in range(2):
                    over_core[k, b, a].wait_recv()

        when(held[k], arrive)

    lane = lax.broadcasted_iota(jnp.int32, (third, LANES), 1)
    rests = []
    for g in range(n):
        for q in range(3):
            acc = jnp.zeros((third, LANES), jnp.float32)
            for cc in range(m):
                u = coul[g, cc, 2 * depth:2 * depth + third].astype(jnp.float32)
                shift = (cc - q) * REST % LANES
                if shift:
                    u = pltpu.roll(u, shift, 1)
                acc = jnp.where((lane >= cc * REST) & (lane < (cc + 1) * REST), u, acc)
            rests.append(acc.astype(jnp.bfloat16))
    rest_all = jnp.concatenate(rests, axis=0)

    own_p.wait()
    for copies in back:
        for cp, _, cond in copies:
            when(cond, cp.wait_recv)

    flat = jnp.concatenate(
        [jnp.concatenate([panel[t // n, t % n] for t in range(c * tiles_k, (c + 1) * tiles_k)], axis=1)
         for c in range(cols)], axis=0)
    rest_out = jnp.dot(flat, rest_all, preferred_element_type=jnp.float32)
    pieces = []
    for cc in range(m):
        weight = jnp.concatenate(
            [coul[:, cc, h * depth:(h + 1) * depth].reshape(n * depth, LANES) for h in range(2)], axis=1)
        pieces.append(jnp.dot(flat, weight, preferred_element_type=jnp.float32))
        pieces.append(rest_out[:, cc * REST:(cc + 1) * REST])
    o_ref[...] = jnp.concatenate(pieces, axis=1)

    for copies in panels + back:
        for cp, cond, _ in copies:
            when(cond, cp.wait_send)
    for k in range(count):

        def sent(k=k):
            over_y[k].wait_send()
            for b in range(2):
                over_x[k, b].wait_send()
                for a in range(2):
                    over_core[k, b, a].wait_send()

        when(held[k], sent)
        if k:
            when(line_if[k], line[k].wait_send)


def fused(n, m, lesser, greater_transposed, coulomb):
    block, _, cols, order = lesser.shape
    depth, width = coulomb.shape
    energies = n * block
    total = cols * order // LANES
    slots = -(-total // n)
    rows = 2 * block
    forward, inverse = tables(energies)
    passes = 2 * (-(-slots // 2))
    places = 1 + 2 * (n // 2 - 1)
    out = pl.pallas_call(
        functools.partial(kernel, n, m),
        out_shape=jax.ShapeDtypeStruct((cols * rows, order), jnp.float32),
        in_specs=[pl.BlockSpec(memory_space=pl.ANY)] * 5,
        out_specs=pl.BlockSpec(memory_space=pltpu.VMEM),
        scratch_shapes=[
            pltpu.VMEM((block, cols, 2, order), jnp.float32),
            pltpu.VMEM((block, cols, 2, order), jnp.float32),
            pltpu.VMEM((depth, width), jnp.bfloat16),
            pltpu.VMEM(forward.shape, jnp.bfloat16),
            pltpu.VMEM(inverse.shape, jnp.bfloat16),
            pltpu.VMEM((n, slots, 3 * rows, LANES), jnp.bfloat16),
            pltpu.VMEM((slots, n, 3 * rows, LANES), jnp.bfloat16),
            pltpu.VMEM((slots, n, rows, LANES), jnp.bfloat16),
            pltpu.VMEM((slots, n, rows, LANES), jnp.bfloat16),
            pltpu.VMEM((n, m, 2 * depth + depth // 3, LANES), jnp.bfloat16),
            pltpu.SemaphoreType.DMA((passes, n)),
            pltpu.SemaphoreType.DMA((passes, n)),
            pltpu.SemaphoreType.DMA((passes, n)),
            pltpu.SemaphoreType.DMA((passes, n)),
            pltpu.SemaphoreType.DMA((8 * places,)),
            pltpu.SemaphoreType.DMA((8 * places,)),
            pltpu.SemaphoreType.DMA((2,)),
            pltpu.SemaphoreType.DMA((5,)),
        ],
        compiler_params=pltpu.CompilerParams(
            collective_id=0, has_side_effects=True, vmem_limit_bytes=63 * 2**20),
        cost_estimate=pl.CostEstimate(flops=2_000_000_000, bytes_accessed=8_000_000, transcendentals=0),
    )(lesser.transpose(0, 2, 1, 3), greater_transposed.transpose(0, 2, 1, 3), coulomb,
      jnp.asarray(forward), jnp.asarray(inverse))
    return out.reshape(cols, block, 2, order).transpose(1, 2, 0, 3)


def solution(mesh):
    placed = (P("energy", None, "col", None), P("energy", None, "col", None), P("energy", "col"))
    n, m = mesh.shape["energy"], mesh.shape["col"]

    def local(lesser, greater_transposed, coulomb):
        depth, width = coulomb.shape
        fits = (m == 4 and n % 2 == 0 and depth % 48 == 0 and width == 2 * LANES + REST
                and lesser.shape[0] % 8 == 0 and lesser.shape[3] % LANES == 0)
        if fits:
            return fused(n, m, lesser, greater_transposed, coulomb)
        return per_device(lesser, greater_transposed, coulomb)

    return jax.shard_map(
        local,
        mesh=mesh,
        in_specs=placed,
        out_specs=P("energy", None, "col", None),
        check_vma=False,
    )
```

```python
import functools
import math

import jax
import jax.numpy as jnp
import ml_dtypes
import numpy as np
from jax import lax
from jax.experimental import pallas as pl
from jax.experimental.pallas import tpu as pltpu
from jax.sharding import PartitionSpec as P

LANES = 128
REST = 32
MESH = pl.DeviceIdType.MESH


def product(left, right):
    return jnp.dot(left, right, precision=lax.Precision.HIGHEST, preferred_element_type=jnp.float32)


def per_device(lesser, greater_transposed, coulomb):
    lesser_all, greater_all = (
        lax.all_to_all(lesser, "energy", split_axis=3, concat_axis=0, tiled=True),
        lax.all_to_all(greater_transposed, "energy", split_axis=3, concat_axis=0, tiled=True),
    )
    energies = lesser_all.shape[0]
    columns_here = lesser_all.shape[2]
    rows_here = lesser_all.shape[3]
    padded = 2 * energies
    lesser_re = lesser_all[:, 0].reshape(energies, -1)
    lesser_im = lesser_all[:, 1].reshape(energies, -1)
    greater_re = greater_all[:, 0].reshape(energies, -1)
    greater_im = greater_all[:, 1].reshape(energies, -1)
    frequency = lax.broadcasted_iota(jnp.int32, (padded, energies), 0)
    position = lax.broadcasted_iota(jnp.int32, (padded, energies), 1)
    phases = frequency * position % padded
    angles = phases.astype(jnp.float32) * (2.0 * math.pi / padded)
    cos_table = jnp.cos(angles)
    sin_table = jnp.sin(angles)
    left_re = product(cos_table, lesser_re) + product(sin_table, lesser_im)
    left_im = product(cos_table, lesser_im) - product(sin_table, lesser_re)
    right_re = product(cos_table, greater_re) - product(sin_table, greater_im)
    right_im = product(cos_table, greater_im) + product(sin_table, greater_re)
    mixed_re = left_re * right_re - left_im * right_im
    mixed_im = left_re * right_im + left_im * right_re
    corr_re = (product(cos_table.T, mixed_re) - product(sin_table.T, mixed_im)) / padded
    corr_im = (product(cos_table.T, mixed_im) + product(sin_table.T, mixed_re)) / padded
    factor = 1.0 / math.sqrt(energies)
    polar_re = (corr_im * factor).reshape(energies, columns_here, rows_here)
    polar_im = (-corr_re * factor).reshape(energies, columns_here, rows_here)
    polarized = jnp.stack([polar_re, polar_im], axis=1).astype(jnp.bfloat16)
    coulomb_wide = lax.all_gather(coulomb, "col", axis=1, tiled=True)
    order = coulomb_wide.shape[1]
    returned = lax.all_to_all(polarized, "energy", split_axis=0, concat_axis=3, tiled=True)
    flattened = returned.reshape(-1, order)
    running = jnp.dot(
        flattened,
        lax.all_gather(coulomb_wide, "energy", axis=0, tiled=True),
        preferred_element_type=jnp.float32,
    )
    screened = running.reshape(returned.shape)
    return screened


def split_table(table):
    high = table.astype(ml_dtypes.bfloat16)
    low = (table - high.astype(np.float64)).astype(ml_dtypes.bfloat16)
    return np.concatenate([high, high, low], axis=1)


def tables(energies):
    padded = 2 * energies
    angle = 2.0 * math.pi / padded * (np.outer(np.arange(padded), np.arange(energies)) % padded)
    cos, sin = np.cos(angle), np.sin(angle)
    forward_re = np.stack([cos, sin], axis=2).reshape(padded, padded)
    forward_im = np.stack([-sin, cos], axis=2).reshape(padded, padded)
    forward = np.concatenate([forward_re, forward_im], axis=0)
    scale = 1.0 / (padded * math.sqrt(energies))
    corr_re = np.concatenate([cos.T, -sin.T], axis=1)
    corr_im = np.concatenate([sin.T, cos.T], axis=1)
    inverse = np.stack([corr_im, -corr_re], axis=1).reshape(padded, 2 * padded) * scale
    return split_table(forward), split_table(inverse)


def high_low(x):
    high = x.astype(jnp.bfloat16)
    return high, (x - high.astype(jnp.float32)).astype(jnp.bfloat16)


def kernel(n, m, l_hbm, r_hbm, w_hbm, tf_hbm, ti_hbm, o_ref, l_ref, r_ref, w_ref, tf_ref, ti_ref,
           give, take, polar, panel, coul, lr_send, lr_recv, p_send, p_recv, c_send, c_recv, own_sem, load_sem):
    here_e, here_c = lax.axis_index("energy"), lax.axis_index("col")
    block, cols, _, order = l_ref.shape
    tiles_k = order // LANES
    total = cols * tiles_k
    full, extra = total // n, total % n
    slots = full + (1 if extra else 0)
    rows = 2 * block
    depth, width = w_ref.shape
    wide = width - REST
    third = depth // 3
    groups = [(start, min(start + 2, slots)) for start in range(0, slots, 2)]

    loads = [pltpu.make_async_copy(a, b, load_sem.at[i]) for i, (a, b) in enumerate(
        [(l_hbm, l_ref), (r_hbm, r_ref), (w_hbm, w_ref), (tf_hbm, tf_ref), (ti_hbm, ti_ref)])]
    for i in (2, 0, 1, 3, 4):
        loads[i].start()

    z, y = here_e // 2, lax.rem(here_e, 2)
    x, core = here_c // 2, lax.rem(here_c, 2)
    nz = n // 2
    peer_y = z * 2 + 1 - y
    peer_x = (1 - x) * 2 + core
    peer_core = x * 2 + 1 - core

    barrier = pltpu.get_barrier_semaphore()
    for s in range(1, n):
        pl.semaphore_signal(barrier, inc=1, device_id={"energy": lax.rem(here_e + s, n)}, device_id_type=MESH)
    for peer in (peer_x, peer_core):
        pl.semaphore_signal(barrier, inc=1, device_id={"col": peer}, device_id_type=MESH)

    sign = jnp.where(lax.broadcasted_iota(jnp.int32, (rows, LANES), 0) % 2 == 0, 1.0, -1.0)

    def pack(t):
        j, d = t // n, t % n
        c, k = t // tiles_k, t % tiles_k
        lanes = slice(k * LANES, (k + 1) * LANES)
        high, low = high_low(l_ref[:, c, :, lanes].reshape(rows, LANES))
        give[d, j, 0:rows] = high
        give[d, j, rows:2 * rows] = low
        right = r_ref[:, c, :, lanes].reshape(rows, LANES) * sign
        give[d, j, 2 * rows:3 * rows] = right.astype(jnp.bfloat16)

    def exchange(source, target, send_sems, recv_sems, send_if, recv_if):
        out = []
        for i, (start, stop) in enumerate(groups):
            copies = []
            for s in range(1, n):
                dev = lax.rem(here_e + s, n)
                whole = min(stop, full) - start
                if whole:
                    copies.append((pltpu.make_async_remote_copy(
                        src_ref=source(start, whole, dev), dst_ref=target(start, whole),
                        send_sem=send_sems.at[2 * i, s], recv_sem=recv_sems.at[2 * i, s],
                        device_id={"energy": dev}, device_id_type=MESH), None, None))
                if stop > full:
                    copies.append((pltpu.make_async_remote_copy(
                        src_ref=source(full, 1, dev), dst_ref=target(full, 1),
                        send_sem=send_sems.at[2 * i + 1, s], recv_sem=recv_sems.at[2 * i + 1, s],
                        device_id={"energy": dev}, device_id_type=MESH), send_if(s), recv_if(s)))
            out.append(copies)
        return out

    def when(cond, f):
        if cond is None:
            f()
        else:
            pl.when(cond)(f)

    panels = exchange(
        lambda a, w, dev: give.at[dev, pl.ds(a, w)], lambda a, w: take.at[pl.ds(a, w), here_e],
        lr_send, lr_recv, lambda s: lax.rem(here_e + s, n) < extra, lambda s: here_e < extra)
    back = exchange(
        lambda a, w, dev: polar.at[pl.ds(a, w), dev], lambda a, w: panel.at[pl.ds(a, w), here_e],
        p_send, p_recv, lambda s: here_e < extra, lambda s: lax.rem(here_e + n - s, n) < extra)

    places = [(0, 0)] + [(way, s) for s in range(1, nz) for way in (1, -1)]

    def share(index, e, c, dev):
        return pltpu.make_async_remote_copy(
            src_ref=coul.at[e, c], dst_ref=coul.at[e, c], send_sem=c_send.at[index],
            recv_sem=c_recv.at[index], device_id=dev, device_id_type=MESH)

    def inside(position):
        return (position >= 0) & (position < nz)

    count = len(places)
    iz, iy, ix, ic = 0, count, 2 * count, 4 * count
    held, line, line_if, over_y, over_x, over_core = {}, {}, {}, {}, {}, {}
    for k, (way, s) in enumerate(places):
        zk = lax.rem(z - way * s + nz, nz)
        held[k] = None if k == 0 else inside(z - way * s)
        owner = (zk * 2 + y, zk * 2 + 1 - y)
        over_y[k] = share(iy + k, owner[0], here_c, {"energy": peer_y})
        for b in range(2):
            over_x[k, b] = share(ix + 2 * k + b, owner[b], here_c, {"col": peer_x})
            for a in range(2):
                over_core[k, b, a] = share(
                    ic + 4 * k + 2 * b + a, owner[b], here_c if a == 0 else peer_x, {"col": peer_core})
        if k:
            before = lax.rem(z - way * (s - 1) + nz, nz)
            line[k] = share(iz + k, before * 2 + y, here_c, {"energy": lax.rem(z + way + nz, nz) * 2 + y})
            line_if[k] = inside(z - way * (s - 1)) & inside(z + way)

    loads[2].wait()
    w = w_ref[...]
    coul[here_e, here_c, 0:depth] = w[:, 0:LANES]
    coul[here_e, here_c, depth:2 * depth] = w[:, LANES:2 * LANES]
    rest = w[:, wide:].astype(jnp.float32)
    packed = jnp.concatenate(
        [rest[q * third:(q + 1) * third] for q in range(3)] + [jnp.zeros((third, LANES - 3 * REST), jnp.float32)],
        axis=1)
    coul[here_e, here_c, 2 * depth:2 * depth + third] = packed.astype(jnp.bfloat16)
    pl.semaphore_wait(barrier, n - 1 + 2)
    for k, (way, s) in enumerate(places):
        if s == 1:
            when(line_if[k], line[k].start)
    over_y[0].start()
    over_x[0, 0].start()
    over_core[0, 0, 0].start()

    loads[0].wait()
    loads[1].wait()
    first = groups[0][1] * n
    for t in range(min(first, total)):
        pack(t)
    for cp, cond, _ in panels[0]:
        when(cond, cp.start)

    for t in range(first, total):
        pack(t)
    for copies in panels[1:]:
        for cp, cond, _ in copies:
            when(cond, cp.start)
    own = pltpu.make_async_copy(give.at[here_e], take.at[:, here_e], own_sem.at[0])
    own.start()

    def relay_z(distance):
        for k, (way, s) in enumerate(places):
            if s != distance:
                continue

            def pass_on(k=k, s=s, way=way):
                line[k].wait_recv()
                if s + 1 < nz:
                    after = places.index((way, s + 1))
                    pl.when(line_if[after])(line[after].start)
                over_y[k].start()
                over_x[k, 0].start()
                over_core[k, 0, 0].start()

            when(held[k], pass_on)

    def relay_y(distance):
        for k, (way, s) in enumerate(places):
            if s != distance:
                continue

            def pass_y(k=k):
                over_y[k].wait_recv()
                over_x[k, 1].start()
                over_core[k, 1, 0].start()

            when(held[k], pass_y)

    span = n * rows

    def correlate(i):
        start, stop = groups[i]
        for cp, _, cond in panels[i]:
            when(cond, cp.wait_recv)

        def piece(p):
            return jnp.concatenate(
                [take[j, :, p * rows:(p + 1) * rows].reshape(span, LANES) for j in range(start, stop)], axis=1)

        l_high, l_low, r_high = piece(0), piece(1), piece(2)
        left = jnp.dot(tf_ref[...], jnp.concatenate([l_high, l_low, l_high], axis=0),
                       preferred_element_type=jnp.float32)
        right = jnp.dot(tf_ref[:, span:], jnp.concatenate([r_high, r_high], axis=0),
                        preferred_element_type=jnp.float32)
        a, b = left[:span], left[span:]
        c, d = right[:span], right[span:]
        mixed = jnp.concatenate([a * c + b * d, b * c - a * d], axis=0)
        m_high, m_low = high_low(mixed)
        polarized = jnp.dot(ti_ref[...], jnp.concatenate([m_high, m_low, m_high], axis=0),
                            preferred_element_type=jnp.float32).astype(jnp.bfloat16)
        for j in range(start, stop):
            polar[j] = polarized[:, (j - start) * LANES:(j - start + 1) * LANES].reshape(n, rows, LANES)
        for cp, cond, _ in back[i]:
            when(cond, cp.start)

    relay_z(1)
    relay_y(0)
    for s in range(2, nz - 1):
        relay_z(s)
        relay_y(s - 1)
    loads[3].wait()
    loads[4].wait()
    own.wait()
    correlate(0)
    if nz > 2:
        relay_z(nz - 1)
        relay_y(nz - 2)
    relay_y(nz - 1)
    for i in range(1, len(groups)):
        correlate(i)
    own_p = pltpu.make_async_copy(polar.at[:, here_e], panel.at[:, here_e], own_sem.at[1])
    own_p.start()

    for k in range(count):

        def pass_x(k=k):
            for b in range(2):
                over_x[k, b].wait_recv()
                over_core[k, b, 1].start()

        when(held[k], pass_x)
    for k in range(count):

        def arrive(k=k):
            for b in range(2):
                for a in range(2):
                    over_core[k, b, a].wait_recv()

        when(held[k], arrive)

    lane = lax.broadcasted_iota(jnp.int32, (third, LANES), 1)
    rests = []
    for g in range(n):
        for q in range(3):
            acc = jnp.zeros((third, LANES), jnp.float32)
            for cc in range(m):
                u = coul[g, cc, 2 * depth:2 * depth + third].astype(jnp.float32)
                shift = (cc - q) * REST % LANES
                if shift:
                    u = pltpu.roll(u, shift, 1)
                acc = jnp.where((lane >= cc * REST) & (lane < (cc + 1) * REST), u, acc)
            rests.append(acc.astype(jnp.bfloat16))
    rest_all = jnp.concatenate(rests, axis=0)

    own_p.wait()
    for copies in back:
        for cp, _, cond in copies:
            when(cond, cp.wait_recv)

    flat = jnp.concatenate(
        [jnp.concatenate([panel[t // n, t % n] for t in range(c * tiles_k, (c + 1) * tiles_k)], axis=1)
         for c in range(cols)], axis=0)
    rest_out = jnp.dot(flat, rest_all, preferred_element_type=jnp.float32)
    pieces = []
    for cc in range(m):
        weight = jnp.concatenate(
            [coul[:, cc, h * depth:(h + 1) * depth].reshape(n * depth, LANES) for h in range(2)], axis=1)
        pieces.append(jnp.dot(flat, weight, preferred_element_type=jnp.float32))
        pieces.append(rest_out[:, cc * REST:(cc + 1) * REST])
    screened = jnp.concatenate(pieces, axis=1)
    for c in range(cols):
        o_ref[:, c] = screened[c * rows:(c + 1) * rows].reshape(block, 2, order)

    for copies in panels + back:
        for cp, cond, _ in copies:
            when(cond, cp.wait_send)
    for k in range(count):

        def sent(k=k):
            over_y[k].wait_send()
            for b in range(2):
                over_x[k, b].wait_send()
                for a in range(2):
                    over_core[k, b, a].wait_send()

        when(held[k], sent)
        if k:
            when(line_if[k], line[k].wait_send)


def fused(n, m, lesser, greater_transposed, coulomb):
    block, _, cols, order = lesser.shape
    depth, width = coulomb.shape
    energies = n * block
    total = cols * order // LANES
    slots = -(-total // n)
    rows = 2 * block
    forward, inverse = tables(energies)
    passes = 2 * (-(-slots // 2))
    places = 1 + 2 * (n // 2 - 1)
    out = pl.pallas_call(
        functools.partial(kernel, n, m),
        out_shape=jax.ShapeDtypeStruct((block, cols, 2, order), jnp.float32),
        in_specs=[pl.BlockSpec(memory_space=pl.ANY)] * 5,
        out_specs=pl.BlockSpec(memory_space=pltpu.VMEM),
        scratch_shapes=[
            pltpu.VMEM((block, cols, 2, order), jnp.float32),
            pltpu.VMEM((block, cols, 2, order), jnp.float32),
            pltpu.VMEM((depth, width), jnp.bfloat16),
            pltpu.VMEM(forward.shape, jnp.bfloat16),
            pltpu.VMEM(inverse.shape, jnp.bfloat16),
            pltpu.VMEM((n, slots, 3 * rows, LANES), jnp.bfloat16),
            pltpu.VMEM((slots, n, 3 * rows, LANES), jnp.bfloat16),
            pltpu.VMEM((slots, n, rows, LANES), jnp.bfloat16),
            pltpu.VMEM((slots, n, rows, LANES), jnp.bfloat16),
            pltpu.VMEM((n, m, 2 * depth + depth // 3, LANES), jnp.bfloat16),
            pltpu.SemaphoreType.DMA((passes, n)),
            pltpu.SemaphoreType.DMA((passes, n)),
            pltpu.SemaphoreType.DMA((passes, n)),
            pltpu.SemaphoreType.DMA((passes, n)),
            pltpu.SemaphoreType.DMA((8 * places,)),
            pltpu.SemaphoreType.DMA((8 * places,)),
            pltpu.SemaphoreType.DMA((2,)),
            pltpu.SemaphoreType.DMA((5,)),
        ],
        compiler_params=pltpu.CompilerParams(
            collective_id=0, has_side_effects=True, vmem_limit_bytes=63 * 2**20),
        cost_estimate=pl.CostEstimate(flops=2_000_000_000, bytes_accessed=8_000_000, transcendentals=0),
    )(lesser.transpose(0, 2, 1, 3), greater_transposed.transpose(0, 2, 1, 3), coulomb,
      jnp.asarray(forward), jnp.asarray(inverse))
    return out.transpose(0, 2, 1, 3)


def solution(mesh):
    placed = (P("energy", None, "col", None), P("energy", None, "col", None), P("energy", "col"))
    n, m = mesh.shape["energy"], mesh.shape["col"]

    def local(lesser, greater_transposed, coulomb):
        depth, width = coulomb.shape
        fits = (m == 4 and n % 2 == 0 and depth % 48 == 0 and width == 2 * LANES + REST
                and lesser.shape[0] % 8 == 0 and lesser.shape[3] % LANES == 0)
        if fits:
            return fused(n, m, lesser, greater_transposed, coulomb)
        return per_device(lesser, greater_transposed, coulomb)

    return jax.shard_map(
        local,
        mesh=mesh,
        in_specs=placed,
        out_specs=P("energy", None, "col", None),
        check_vma=False,
    )
```

```python
import functools
import math

import jax
import jax.numpy as jnp
import ml_dtypes
import numpy as np
from jax import lax
from jax.experimental import pallas as pl
from jax.experimental.pallas import tpu as pltpu
from jax.sharding import PartitionSpec as P

LANES = 128
REST = 32
MESH = pl.DeviceIdType.MESH


def product(left, right):
    return jnp.dot(left, right, precision=lax.Precision.HIGHEST, preferred_element_type=jnp.float32)


def per_device(lesser, greater_transposed, coulomb):
    lesser_all, greater_all = (
        lax.all_to_all(lesser, "energy", split_axis=3, concat_axis=0, tiled=True),
        lax.all_to_all(greater_transposed, "energy", split_axis=3, concat_axis=0, tiled=True),
    )
    energies = lesser_all.shape[0]
    columns_here = lesser_all.shape[2]
    rows_here = lesser_all.shape[3]
    padded = 2 * energies
    lesser_re = lesser_all[:, 0].reshape(energies, -1)
    lesser_im = lesser_all[:, 1].reshape(energies, -1)
    greater_re = greater_all[:, 0].reshape(energies, -1)
    greater_im = greater_all[:, 1].reshape(energies, -1)
    frequency = lax.broadcasted_iota(jnp.int32, (padded, energies), 0)
    position = lax.broadcasted_iota(jnp.int32, (padded, energies), 1)
    phases = frequency * position % padded
    angles = phases.astype(jnp.float32) * (2.0 * math.pi / padded)
    cos_table = jnp.cos(angles)
    sin_table = jnp.sin(angles)
    left_re = product(cos_table, lesser_re) + product(sin_table, lesser_im)
    left_im = product(cos_table, lesser_im) - product(sin_table, lesser_re)
    right_re = product(cos_table, greater_re) - product(sin_table, greater_im)
    right_im = product(cos_table, greater_im) + product(sin_table, greater_re)
    mixed_re = left_re * right_re - left_im * right_im
    mixed_im = left_re * right_im + left_im * right_re
    corr_re = (product(cos_table.T, mixed_re) - product(sin_table.T, mixed_im)) / padded
    corr_im = (product(cos_table.T, mixed_im) + product(sin_table.T, mixed_re)) / padded
    factor = 1.0 / math.sqrt(energies)
    polar_re = (corr_im * factor).reshape(energies, columns_here, rows_here)
    polar_im = (-corr_re * factor).reshape(energies, columns_here, rows_here)
    polarized = jnp.stack([polar_re, polar_im], axis=1).astype(jnp.bfloat16)
    coulomb_wide = lax.all_gather(coulomb, "col", axis=1, tiled=True)
    order = coulomb_wide.shape[1]
    returned = lax.all_to_all(polarized, "energy", split_axis=0, concat_axis=3, tiled=True)
    flattened = returned.reshape(-1, order)
    running = jnp.dot(
        flattened,
        lax.all_gather(coulomb_wide, "energy", axis=0, tiled=True),
        preferred_element_type=jnp.float32,
    )
    screened = running.reshape(returned.shape)
    return screened


def split_table(table):
    high = table.astype(ml_dtypes.bfloat16)
    low = (table - high.astype(np.float64)).astype(ml_dtypes.bfloat16)
    return np.concatenate([high, high, low], axis=1)


def tables(energies):
    padded = 2 * energies
    angle = 2.0 * math.pi / padded * (np.outer(np.arange(padded), np.arange(energies)) % padded)
    cos, sin = np.cos(angle), np.sin(angle)
    forward_re = np.stack([cos, sin], axis=2).reshape(padded, padded)
    forward_im = np.stack([-sin, cos], axis=2).reshape(padded, padded)
    forward = np.concatenate([forward_re, forward_im], axis=0)
    scale = 1.0 / (padded * math.sqrt(energies))
    corr_re = np.concatenate([cos.T, -sin.T], axis=1)
    corr_im = np.concatenate([sin.T, cos.T], axis=1)
    inverse = np.stack([corr_im, -corr_re], axis=1).reshape(padded, 2 * padded) * scale
    return split_table(forward), split_table(inverse)


def high_low(x):
    high = x.astype(jnp.bfloat16)
    return high, (x - high.astype(jnp.float32)).astype(jnp.bfloat16)


def kernel(n, m, l_hbm, r_hbm, w_hbm, tf_hbm, ti_hbm, o_ref, l_ref, r_ref, w_ref, tf_ref, ti_ref,
           give, take, polar, panel, coul, lr_send, lr_recv, p_send, p_recv, c_send, c_recv, own_sem, load_sem):
    here_e, here_c = lax.axis_index("energy"), lax.axis_index("col")
    block, cols, _, order = l_ref.shape
    tiles_k = order // LANES
    total = cols * tiles_k
    full, extra = total // n, total % n
    slots = full + (1 if extra else 0)
    rows = 2 * block
    depth, width = w_ref.shape
    wide = width - REST
    third = depth // 3
    lead = 1 if extra else 0
    groups = [(0, slots - 1), (slots - 1, slots)] if slots > 1 else [(0, 1)]

    def slot(t):
        return (0, t) if t < extra else ((t - extra) // n + lead, (t - extra) % n)


    loads = [pltpu.make_async_copy(a, b, load_sem.at[i]) for i, (a, b) in enumerate(
        [(l_hbm, l_ref), (r_hbm, r_ref), (w_hbm, w_ref), (tf_hbm, tf_ref), (ti_hbm, ti_ref)])]
    for i in (2, 0, 1, 3, 4):
        loads[i].start()

    z, y = here_e // 2, lax.rem(here_e, 2)
    x, core = here_c // 2, lax.rem(here_c, 2)
    nz = n // 2
    peer_y = z * 2 + 1 - y
    peer_x = (1 - x) * 2 + core
    peer_core = x * 2 + 1 - core

    barrier = pltpu.get_barrier_semaphore()
    for s in range(1, n):
        pl.semaphore_signal(barrier, inc=1, device_id={"energy": lax.rem(here_e + s, n)}, device_id_type=MESH)
    for peer in (peer_x, peer_core):
        pl.semaphore_signal(barrier, inc=1, device_id={"col": peer}, device_id_type=MESH)

    sign = jnp.where(lax.broadcasted_iota(jnp.int32, (rows, LANES), 0) % 2 == 0, 1.0, -1.0)

    def pack(t):
        j, d = slot(t)
        c, k = t % cols, t // cols
        lanes = slice(k * LANES, (k + 1) * LANES)
        high, low = high_low(l_ref[:, c, :, lanes].reshape(rows, LANES))
        give[d, j, 0:rows] = high
        give[d, j, rows:2 * rows] = low
        right = r_ref[:, c, :, lanes].reshape(rows, LANES) * sign
        give[d, j, 2 * rows:3 * rows] = right.astype(jnp.bfloat16)

    def exchange(source, target, send_sems, recv_sems, send_if, recv_if):
        out = []
        for i, (start, stop) in enumerate(groups):
            copies = []
            for s in range(1, n):
                dev = lax.rem(here_e + s, n)
                begin = max(start, lead)
                if stop > begin:
                    copies.append((pltpu.make_async_remote_copy(
                        src_ref=source(begin, stop - begin, dev), dst_ref=target(begin, stop - begin),
                        send_sem=send_sems.at[2 * i, s], recv_sem=recv_sems.at[2 * i, s],
                        device_id={"energy": dev}, device_id_type=MESH), None, None))
                if start < lead:
                    copies.append((pltpu.make_async_remote_copy(
                        src_ref=source(0, 1, dev), dst_ref=target(0, 1),
                        send_sem=send_sems.at[2 * i + 1, s], recv_sem=recv_sems.at[2 * i + 1, s],
                        device_id={"energy": dev}, device_id_type=MESH), send_if(s), recv_if(s)))
            out.append(copies)
        return out

    def when(cond, f):
        if cond is None:
            f()
        else:
            pl.when(cond)(f)

    panels = exchange(
        lambda a, w, dev: give.at[dev, pl.ds(a, w)], lambda a, w: take.at[pl.ds(a, w), here_e],
        lr_send, lr_recv, lambda s: lax.rem(here_e + s, n) < extra, lambda s: here_e < extra)
    back = exchange(
        lambda a, w, dev: polar.at[pl.ds(a, w), dev], lambda a, w: panel.at[pl.ds(a, w), here_e],
        p_send, p_recv, lambda s: here_e < extra, lambda s: lax.rem(here_e + n - s, n) < extra)

    places = [(0, 0)] + [(way, s) for s in range(1, nz) for way in (1, -1)]

    def share(index, e, c, dev):
        return pltpu.make_async_remote_copy(
            src_ref=coul.at[e, c], dst_ref=coul.at[e, c], send_sem=c_send.at[index],
            recv_sem=c_recv.at[index], device_id=dev, device_id_type=MESH)

    def inside(position):
        return (position >= 0) & (position < nz)

    count = len(places)
    iz, iy, ix, ic = 0, count, 2 * count, 4 * count
    held, line, line_if, over_y, over_x, over_core = {}, {}, {}, {}, {}, {}
    for k, (way, s) in enumerate(places):
        zk = lax.rem(z - way * s + nz, nz)
        held[k] = None if k == 0 else inside(z - way * s)
        owner = (zk * 2 + y, zk * 2 + 1 - y)
        over_y[k] = share(iy + k, owner[0], here_c, {"energy": peer_y})
        for b in range(2):
            over_x[k, b] = share(ix + 2 * k + b, owner[b], here_c, {"col": peer_x})
            for a in range(2):
                over_core[k, b, a] = share(
                    ic + 4 * k + 2 * b + a, owner[b], here_c if a == 0 else peer_x, {"col": peer_core})
        if k:
            before = lax.rem(z - way * (s - 1) + nz, nz)
            line[k] = share(iz + k, before * 2 + y, here_c, {"energy": lax.rem(z + way + nz, nz) * 2 + y})
            line_if[k] = inside(z - way * (s - 1)) & inside(z + way)

    loads[2].wait()
    w = w_ref[...]
    coul[here_e, here_c, 0:depth] = w[:, 0:LANES]
    coul[here_e, here_c, depth:2 * depth] = w[:, LANES:2 * LANES]
    rest = w[:, wide:].astype(jnp.float32)
    packed = jnp.concatenate(
        [rest[q * third:(q + 1) * third] for q in range(3)] + [jnp.zeros((third, LANES - 3 * REST), jnp.float32)],
        axis=1)
    coul[here_e, here_c, 2 * depth:2 * depth + third] = packed.astype(jnp.bfloat16)
    pl.semaphore_wait(barrier, n - 1 + 2)
    for k, (way, s) in enumerate(places):
        if s == 1:
            when(line_if[k], line[k].start)
    over_y[0].start()
    over_x[0, 0].start()
    over_core[0, 0, 0].start()

    loads[0].wait()
    loads[1].wait()
    first = extra + (groups[0][1] - lead) * n
    for t in range(first):
        pack(t)
    for cp, cond, _ in panels[0]:
        when(cond, cp.start)

    for t in range(first, total):
        pack(t)
    for copies in panels[1:]:
        for cp, cond, _ in copies:
            when(cond, cp.start)
    own = pltpu.make_async_copy(give.at[here_e], take.at[:, here_e], own_sem.at[0])
    own.start()

    def relay_z(distance):
        for k, (way, s) in enumerate(places):
            if s != distance:
                continue

            def pass_on(k=k, s=s, way=way):
                line[k].wait_recv()
                if s + 1 < nz:
                    after = places.index((way, s + 1))
                    pl.when(line_if[after])(line[after].start)
                over_y[k].start()
                over_x[k, 0].start()
                over_core[k, 0, 0].start()

            when(held[k], pass_on)

    def relay_y(distance):
        for k, (way, s) in enumerate(places):
            if s != distance:
                continue

            def pass_y(k=k):
                over_y[k].wait_recv()
                over_x[k, 1].start()
                over_core[k, 1, 0].start()

            when(held[k], pass_y)

    span = n * rows

    def correlate(i):
        start, stop = groups[i]
        for cp, _, cond in panels[i]:
            when(cond, cp.wait_recv)

        def piece(p):
            return jnp.concatenate(
                [take[j, :, p * rows:(p + 1) * rows].reshape(span, LANES) for j in range(start, stop)], axis=1)

        l_high, l_low, r_high = piece(0), piece(1), piece(2)
        left = jnp.dot(tf_ref[...], jnp.concatenate([l_high, l_low, l_high], axis=0),
                       preferred_element_type=jnp.float32)
        right = jnp.dot(tf_ref[:, span:], jnp.concatenate([r_high, r_high], axis=0),
                        preferred_element_type=jnp.float32)
        a, b = left[:span], left[span:]
        c, d = right[:span], right[span:]
        mixed = jnp.concatenate([a * c + b * d, b * c - a * d], axis=0)
        m_high, m_low = high_low(mixed)
        polarized = jnp.dot(ti_ref[...], jnp.concatenate([m_high, m_low, m_high], axis=0),
                            preferred_element_type=jnp.float32).astype(jnp.bfloat16)
        for j in range(start, stop):
            polar[j] = polarized[:, (j - start) * LANES:(j - start + 1) * LANES].reshape(n, rows, LANES)
        for cp, cond, _ in back[i]:
            when(cond, cp.start)

    relay_z(1)
    relay_y(0)
    for s in range(2, nz - 1):
        relay_z(s)
        relay_y(s - 1)
    loads[3].wait()
    loads[4].wait()
    own.wait()
    correlate(0)
    if nz > 2:
        relay_z(nz - 1)
        relay_y(nz - 2)
    relay_y(nz - 1)
    for i in range(1, len(groups)):
        correlate(i)
    own_p = pltpu.make_async_copy(polar.at[:, here_e], panel.at[:, here_e], own_sem.at[1])
    own_p.start()

    for k in range(count):

        def pass_x(k=k):
            for b in range(2):
                over_x[k, b].wait_recv()
                over_core[k, b, 1].start()

        when(held[k], pass_x)
    for k in range(count):

        def arrive(k=k):
            for b in range(2):
                for a in range(2):
                    over_core[k, b, a].wait_recv()

        when(held[k], arrive)

    lane = lax.broadcasted_iota(jnp.int32, (third, LANES), 1)
    rests = []
    for g in range(n):
        for q in range(3):
            acc = jnp.zeros((third, LANES), jnp.float32)
            for cc in range(m):
                u = coul[g, cc, 2 * depth:2 * depth + third].astype(jnp.float32)
                shift = (cc - q) * REST % LANES
                if shift:
                    u = pltpu.roll(u, shift, 1)
                acc = jnp.where((lane >= cc * REST) & (lane < (cc + 1) * REST), u, acc)
            rests.append(acc.astype(jnp.bfloat16))
    rest_all = jnp.concatenate(rests, axis=0)

    def multiply(low, high):
        flat = jnp.concatenate(
            [jnp.concatenate([panel[slot(k * cols + c)] for k in range(low, high)], axis=1) for c in range(cols)],
            axis=0)
        part = slice(low * LANES, high * LANES)
        out = []
        for cc in range(m):
            weight = jnp.concatenate(
                [coul[:, cc, h * depth:(h + 1) * depth].reshape(n * depth, LANES)[part] for h in range(2)], axis=1)
            out.append(jnp.dot(flat, weight, preferred_element_type=jnp.float32))
        out.append(jnp.dot(flat, rest_all[part], preferred_element_type=jnp.float32))
        return out

    own_p.wait()
    cut = first // cols
    sums = None
    for i, copies in enumerate(back):
        for cp, _, cond in copies:
            when(cond, cp.wait_recv)
        low, high = (0 if i == 0 else cut), (tiles_k if i == len(back) - 1 else cut)
        if high > low:
            terms = multiply(low, high)
            sums = terms if sums is None else [p + q for p, q in zip(sums, terms)]
    pieces = []
    for cc in range(m):
        pieces.append(sums[cc])
        pieces.append(sums[m][:, cc * REST:(cc + 1) * REST])
    screened = jnp.concatenate(pieces, axis=1)
    for c in range(cols):
        o_ref[:, c] = screened[c * rows:(c + 1) * rows].reshape(block, 2, order)

    for copies in panels + back:
        for cp, cond, _ in copies:
            when(cond, cp.wait_send)
    for k in range(count):

        def sent(k=k):
            over_y[k].wait_send()
            for b in range(2):
                over_x[k, b].wait_send()
                for a in range(2):
                    over_core[k, b, a].wait_send()

        when(held[k], sent)
        if k:
            when(line_if[k], line[k].wait_send)


def fused(n, m, lesser, greater_transposed, coulomb):
    block, _, cols, order = lesser.shape
    depth, width = coulomb.shape
    energies = n * block
    total = cols * order // LANES
    slots = -(-total // n)
    rows = 2 * block
    forward, inverse = tables(energies)
    passes = 4
    places = 1 + 2 * (n // 2 - 1)
    out = pl.pallas_call(
        functools.partial(kernel, n, m),
        out_shape=jax.ShapeDtypeStruct((block, cols, 2, order), jnp.float32),
        in_specs=[pl.BlockSpec(memory_space=pl.ANY)] * 5,
        out_specs=pl.BlockSpec(memory_space=pltpu.VMEM),
        scratch_shapes=[
            pltpu.VMEM((block, cols, 2, order), jnp.float32),
            pltpu.VMEM((block, cols, 2, order), jnp.float32),
            pltpu.VMEM((depth, width), jnp.bfloat16),
            pltpu.VMEM(forward.shape, jnp.bfloat16),
            pltpu.VMEM(inverse.shape, jnp.bfloat16),
            pltpu.VMEM((n, slots, 3 * rows, LANES), jnp.bfloat16),
            pltpu.VMEM((slots, n, 3 * rows, LANES), jnp.bfloat16),
            pltpu.VMEM((slots, n, rows, LANES), jnp.bfloat16),
            pltpu.VMEM((slots, n, rows, LANES), jnp.bfloat16),
            pltpu.VMEM((n, m, 2 * depth + depth // 3, LANES), jnp.bfloat16),
            pltpu.SemaphoreType.DMA((passes, n)),
            pltpu.SemaphoreType.DMA((passes, n)),
            pltpu.SemaphoreType.DMA((passes, n)),
            pltpu.SemaphoreType.DMA((passes, n)),
            pltpu.SemaphoreType.DMA((8 * places,)),
            pltpu.SemaphoreType.DMA((8 * places,)),
            pltpu.SemaphoreType.DMA((2,)),
            pltpu.SemaphoreType.DMA((5,)),
        ],
        compiler_params=pltpu.CompilerParams(
            collective_id=0, has_side_effects=True, vmem_limit_bytes=63 * 2**20),
        cost_estimate=pl.CostEstimate(flops=2_000_000_000, bytes_accessed=8_000_000, transcendentals=0),
    )(lesser.transpose(0, 2, 1, 3), greater_transposed.transpose(0, 2, 1, 3), coulomb,
      jnp.asarray(forward), jnp.asarray(inverse))
    return out.transpose(0, 2, 1, 3)


def solution(mesh):
    placed = (P("energy", None, "col", None), P("energy", None, "col", None), P("energy", "col"))
    n, m = mesh.shape["energy"], mesh.shape["col"]

    def local(lesser, greater_transposed, coulomb):
        depth, width = coulomb.shape
        fits = (m == 4 and n % 2 == 0 and depth % 48 == 0 and width == 2 * LANES + REST
                and lesser.shape[0] % 8 == 0 and lesser.shape[3] % LANES == 0)
        if fits:
            return fused(n, m, lesser, greater_transposed, coulomb)
        return per_device(lesser, greater_transposed, coulomb)

    return jax.shard_map(
        local,
        mesh=mesh,
        in_specs=placed,
        out_specs=P("energy", None, "col", None),
        check_vma=False,
    )
```

```python
import functools
import math

import jax
import jax.numpy as jnp
import ml_dtypes
import numpy as np
from jax import lax
from jax.experimental import pallas as pl
from jax.experimental.pallas import tpu as pltpu
from jax.sharding import PartitionSpec as P

LANES = 128
REST = 32
MESH = pl.DeviceIdType.MESH


def product(left, right):
    return jnp.dot(left, right, precision=lax.Precision.HIGHEST, preferred_element_type=jnp.float32)


def per_device(lesser, greater_transposed, coulomb):
    lesser_all, greater_all = (
        lax.all_to_all(lesser, "energy", split_axis=3, concat_axis=0, tiled=True),
        lax.all_to_all(greater_transposed, "energy", split_axis=3, concat_axis=0, tiled=True),
    )
    energies = lesser_all.shape[0]
    columns_here = lesser_all.shape[2]
    rows_here = lesser_all.shape[3]
    padded = 2 * energies
    lesser_re = lesser_all[:, 0].reshape(energies, -1)
    lesser_im = lesser_all[:, 1].reshape(energies, -1)
    greater_re = greater_all[:, 0].reshape(energies, -1)
    greater_im = greater_all[:, 1].reshape(energies, -1)
    frequency = lax.broadcasted_iota(jnp.int32, (padded, energies), 0)
    position = lax.broadcasted_iota(jnp.int32, (padded, energies), 1)
    phases = frequency * position % padded
    angles = phases.astype(jnp.float32) * (2.0 * math.pi / padded)
    cos_table = jnp.cos(angles)
    sin_table = jnp.sin(angles)
    left_re = product(cos_table, lesser_re) + product(sin_table, lesser_im)
    left_im = product(cos_table, lesser_im) - product(sin_table, lesser_re)
    right_re = product(cos_table, greater_re) - product(sin_table, greater_im)
    right_im = product(cos_table, greater_im) + product(sin_table, greater_re)
    mixed_re = left_re * right_re - left_im * right_im
    mixed_im = left_re * right_im + left_im * right_re
    corr_re = (product(cos_table.T, mixed_re) - product(sin_table.T, mixed_im)) / padded
    corr_im = (product(cos_table.T, mixed_im) + product(sin_table.T, mixed_re)) / padded
    factor = 1.0 / math.sqrt(energies)
    polar_re = (corr_im * factor).reshape(energies, columns_here, rows_here)
    polar_im = (-corr_re * factor).reshape(energies, columns_here, rows_here)
    polarized = jnp.stack([polar_re, polar_im], axis=1).astype(jnp.bfloat16)
    coulomb_wide = lax.all_gather(coulomb, "col", axis=1, tiled=True)
    order = coulomb_wide.shape[1]
    returned = lax.all_to_all(polarized, "energy", split_axis=0, concat_axis=3, tiled=True)
    flattened = returned.reshape(-1, order)
    running = jnp.dot(
        flattened,
        lax.all_gather(coulomb_wide, "energy", axis=0, tiled=True),
        preferred_element_type=jnp.float32,
    )
    screened = running.reshape(returned.shape)
    return screened


def split_table(table):
    high = table.astype(ml_dtypes.bfloat16)
    low = (table - high.astype(np.float64)).astype(ml_dtypes.bfloat16)
    return np.concatenate([high, high, low], axis=1)


def tables(energies):
    padded = 2 * energies
    angle = 2.0 * math.pi / padded * (np.outer(np.arange(padded), np.arange(energies)) % padded)
    cos, sin = np.cos(angle), np.sin(angle)
    forward_re = np.stack([cos, sin], axis=2).reshape(padded, padded)
    forward_im = np.stack([-sin, cos], axis=2).reshape(padded, padded)
    forward = np.concatenate([forward_re, forward_im], axis=0)
    scale = 1.0 / (padded * math.sqrt(energies))
    corr_re = np.concatenate([cos.T, -sin.T], axis=1)
    corr_im = np.concatenate([sin.T, cos.T], axis=1)
    inverse = np.stack([corr_im, -corr_re], axis=1).reshape(padded, 2 * padded) * scale
    return split_table(forward), split_table(inverse)


def high_low(x):
    high = x.astype(jnp.bfloat16)
    return high, (x - high.astype(jnp.float32)).astype(jnp.bfloat16)


def kernel(n, m, l_hbm, r_hbm, w_hbm, tf_hbm, ti_hbm, o_ref, l_ref, r_ref, w_ref, tf_ref, ti_ref,
           give, take, polar, panel, coul, lr_send, lr_recv, p_send, p_recv, c_send, c_recv, own_sem, load_sem):
    here_e, here_c = lax.axis_index("energy"), lax.axis_index("col")
    block, cols, _, order = l_ref.shape
    tiles_k = order // LANES
    total = cols * tiles_k
    full, extra = total // n, total % n
    slots = full + (1 if extra else 0)
    rows = 2 * block
    depth, width = w_ref.shape
    wide = width - REST
    third = depth // 3
    lead = 1 if extra else 0
    groups = [(0, slots - 1), (slots - 1, slots)] if slots > 1 else [(0, 1)]

    def slot(t):
        return (0, t) if t < extra else ((t - extra) // n + lead, (t - extra) % n)


    loads = [pltpu.make_async_copy(a, b, load_sem.at[i]) for i, (a, b) in enumerate(
        [(l_hbm, l_ref), (r_hbm, r_ref), (w_hbm, w_ref), (tf_hbm, tf_ref), (ti_hbm, ti_ref)])]
    for i in (2, 0, 1, 3, 4):
        loads[i].start()

    z, y = here_e // 2, lax.rem(here_e, 2)
    x, core = here_c // 2, lax.rem(here_c, 2)
    nz = n // 2
    peer_y = z * 2 + 1 - y
    peer_x = (1 - x) * 2 + core
    peer_core = x * 2 + 1 - core

    barrier = pltpu.get_barrier_semaphore()
    for s in range(1, n):
        pl.semaphore_signal(barrier, inc=1, device_id={"energy": lax.rem(here_e + s, n)}, device_id_type=MESH)
    for peer in (peer_x, peer_core):
        pl.semaphore_signal(barrier, inc=1, device_id={"col": peer}, device_id_type=MESH)

    sign = jnp.where(lax.broadcasted_iota(jnp.int32, (rows, LANES), 0) % 2 == 0, 1.0, -1.0)

    def pack(t):
        j, d = slot(t)
        c, k = t % cols, t // cols
        lanes = slice(k * LANES, (k + 1) * LANES)
        high, low = high_low(l_ref[:, c, :, lanes].reshape(rows, LANES))
        give[d, j, 0:rows] = high
        give[d, j, rows:2 * rows] = low
        right = r_ref[:, c, :, lanes].reshape(rows, LANES) * sign
        give[d, j, 2 * rows:3 * rows] = right.astype(jnp.bfloat16)

    def exchange(source, target, send_sems, recv_sems, send_if, recv_if):
        out = []
        for i, (start, stop) in enumerate(groups):
            copies = []
            for s in range(1, n):
                dev = lax.rem(here_e + s, n)
                begin = max(start, lead)
                if stop > begin:
                    copies.append((pltpu.make_async_remote_copy(
                        src_ref=source(begin, stop - begin, dev), dst_ref=target(begin, stop - begin),
                        send_sem=send_sems.at[2 * i, s], recv_sem=recv_sems.at[2 * i, s],
                        device_id={"energy": dev}, device_id_type=MESH), None, None))
                if start < lead:
                    copies.append((pltpu.make_async_remote_copy(
                        src_ref=source(0, 1, dev), dst_ref=target(0, 1),
                        send_sem=send_sems.at[2 * i + 1, s], recv_sem=recv_sems.at[2 * i + 1, s],
                        device_id={"energy": dev}, device_id_type=MESH), send_if(s), recv_if(s)))
            out.append(copies)
        return out

    def when(cond, f):
        if cond is None:
            f()
        else:
            pl.when(cond)(f)

    panels = exchange(
        lambda a, w, dev: give.at[dev, pl.ds(a, w)], lambda a, w: take.at[pl.ds(a, w), here_e],
        lr_send, lr_recv, lambda s: lax.rem(here_e + s, n) < extra, lambda s: here_e < extra)
    back = exchange(
        lambda a, w, dev: polar.at[pl.ds(a, w), dev], lambda a, w: panel.at[pl.ds(a, w), here_e],
        p_send, p_recv, lambda s: here_e < extra, lambda s: lax.rem(here_e + n - s, n) < extra)

    places = [(0, 0)] + [(way, s) for s in range(1, nz) for way in (1, -1)]

    def share(index, e, c, dev):
        return pltpu.make_async_remote_copy(
            src_ref=coul.at[e, c], dst_ref=coul.at[e, c], send_sem=c_send.at[index],
            recv_sem=c_recv.at[index], device_id=dev, device_id_type=MESH)

    def inside(position):
        return (position >= 0) & (position < nz)

    count = len(places)
    iz, iy, ix, ic = 0, count, 2 * count, 4 * count
    held, line, line_if, over_y, over_x, over_core = {}, {}, {}, {}, {}, {}
    for k, (way, s) in enumerate(places):
        zk = lax.rem(z - way * s + nz, nz)
        held[k] = None if k == 0 else inside(z - way * s)
        owner = (zk * 2 + y, zk * 2 + 1 - y)
        over_y[k] = share(iy + k, owner[0], here_c, {"energy": peer_y})
        for b in range(2):
            over_x[k, b] = share(ix + 2 * k + b, owner[b], here_c, {"col": peer_x})
            for a in range(2):
                over_core[k, b, a] = share(
                    ic + 4 * k + 2 * b + a, owner[b], here_c if a == 0 else peer_x, {"col": peer_core})
        if k:
            before = lax.rem(z - way * (s - 1) + nz, nz)
            line[k] = share(iz + k, before * 2 + y, here_c, {"energy": lax.rem(z + way + nz, nz) * 2 + y})
            line_if[k] = inside(z - way * (s - 1)) & inside(z + way)

    loads[2].wait()
    w = w_ref[...]
    coul[here_e, here_c, 0:depth] = w[:, 0:LANES]
    coul[here_e, here_c, depth:2 * depth] = w[:, LANES:2 * LANES]
    rest = w[:, wide:].astype(jnp.float32)
    packed = jnp.concatenate(
        [rest[q * third:(q + 1) * third] for q in range(3)] + [jnp.zeros((third, LANES - 3 * REST), jnp.float32)],
        axis=1)
    coul[here_e, here_c, 2 * depth:2 * depth + third] = packed.astype(jnp.bfloat16)
    pl.semaphore_wait(barrier, n - 1 + 2)
    for k, (way, s) in enumerate(places):
        if s == 1:
            when(line_if[k], line[k].start)
    over_y[0].start()
    over_x[0, 0].start()
    over_core[0, 0, 0].start()

    loads[0].wait()
    loads[1].wait()
    first = extra + (groups[0][1] - lead) * n
    for t in range(first):
        pack(t)
    for cp, cond, _ in panels[0]:
        when(cond, cp.start)

    for t in range(first, total):
        pack(t)
    for copies in panels[1:]:
        for cp, cond, _ in copies:
            when(cond, cp.start)
    own = pltpu.make_async_copy(give.at[here_e], take.at[:, here_e], own_sem.at[0])
    own.start()

    def relay_z(distance):
        for k, (way, s) in enumerate(places):
            if s != distance:
                continue

            def pass_on(k=k, s=s, way=way):
                line[k].wait_recv()
                if s + 1 < nz:
                    after = places.index((way, s + 1))
                    pl.when(line_if[after])(line[after].start)
                over_y[k].start()
                over_x[k, 0].start()
                over_core[k, 0, 0].start()

            when(held[k], pass_on)

    def relay_y(distance):
        for k, (way, s) in enumerate(places):
            if s != distance:
                continue

            def pass_y(k=k):
                over_y[k].wait_recv()
                over_x[k, 1].start()
                over_core[k, 1, 0].start()

            when(held[k], pass_y)

    def relay_x(distance):
        for k, (way, s) in enumerate(places):
            if s != distance:
                continue

            def pass_x(k=k):
                for b in range(2):
                    over_x[k, b].wait_recv()
                    over_core[k, b, 1].start()

            when(held[k], pass_x)

    span = n * rows

    def correlate(i):
        start, stop = groups[i]
        for cp, _, cond in panels[i]:
            when(cond, cp.wait_recv)

        def piece(p):
            return jnp.concatenate(
                [take[j, :, p * rows:(p + 1) * rows].reshape(span, LANES) for j in range(start, stop)], axis=1)

        l_high, l_low, r_high = piece(0), piece(1), piece(2)
        left = jnp.dot(tf_ref[...], jnp.concatenate([l_high, l_low, l_high], axis=0),
                       preferred_element_type=jnp.float32)
        right = jnp.dot(tf_ref[:, span:], jnp.concatenate([r_high, r_high], axis=0),
                        preferred_element_type=jnp.float32)
        a, b = left[:span], left[span:]
        c, d = right[:span], right[span:]
        mixed = jnp.concatenate([a * c + b * d, b * c - a * d], axis=0)
        m_high, m_low = high_low(mixed)
        polarized = jnp.dot(ti_ref[...], jnp.concatenate([m_high, m_low, m_high], axis=0),
                            preferred_element_type=jnp.float32).astype(jnp.bfloat16)
        for j in range(start, stop):
            polar[j] = polarized[:, (j - start) * LANES:(j - start + 1) * LANES].reshape(n, rows, LANES)
        for cp, cond, _ in back[i]:
            when(cond, cp.start)

    relay_z(1)
    relay_y(0)
    for s in range(2, nz - 1):
        relay_z(s)
        relay_y(s - 1)
    loads[3].wait()
    loads[4].wait()
    own.wait()
    correlate(0)
    if nz > 2:
        relay_z(nz - 1)
        relay_y(nz - 2)
    relay_y(nz - 1)
    for s in range(min(2, nz)):
        relay_x(s)
    for i in range(1, len(groups)):
        correlate(i)
    own_p = pltpu.make_async_copy(polar.at[:, here_e], panel.at[:, here_e], own_sem.at[1])
    own_p.start()

    for s in range(2, nz):
        relay_x(s)
    for k in range(count):

        def arrive(k=k):
            for b in range(2):
                for a in range(2):
                    over_core[k, b, a].wait_recv()

        when(held[k], arrive)

    lane = lax.broadcasted_iota(jnp.int32, (third, LANES), 1)
    rests = []
    for g in range(n):
        for q in range(3):
            acc = jnp.zeros((third, LANES), jnp.float32)
            for cc in range(m):
                u = coul[g, cc, 2 * depth:2 * depth + third].astype(jnp.float32)
                shift = (cc - q) * REST % LANES
                if shift:
                    u = pltpu.roll(u, shift, 1)
                acc = jnp.where((lane >= cc * REST) & (lane < (cc + 1) * REST), u, acc)
            rests.append(acc.astype(jnp.bfloat16))
    rest_all = jnp.concatenate(rests, axis=0)

    def multiply(low, high):
        flat = jnp.concatenate(
            [jnp.concatenate([panel[slot(k * cols + c)] for k in range(low, high)], axis=1) for c in range(cols)],
            axis=0)
        part = slice(low * LANES, high * LANES)
        out = []
        for cc in range(m):
            weight = jnp.concatenate(
                [coul[:, cc, h * depth:(h + 1) * depth].reshape(n * depth, LANES)[part] for h in range(2)], axis=1)
            out.append(jnp.dot(flat, weight, preferred_element_type=jnp.float32))
        out.append(jnp.dot(flat, rest_all[part], preferred_element_type=jnp.float32))
        return out

    own_p.wait()
    cut = first // cols
    sums = None
    for i, copies in enumerate(back):
        for cp, _, cond in copies:
            when(cond, cp.wait_recv)
        low, high = (0 if i == 0 else cut), (tiles_k if i == len(back) - 1 else cut)
        if high > low:
            terms = multiply(low, high)
            sums = terms if sums is None else [p + q for p, q in zip(sums, terms)]
    pieces = []
    for cc in range(m):
        pieces.append(sums[cc])
        pieces.append(sums[m][:, cc * REST:(cc + 1) * REST])
    screened = jnp.concatenate(pieces, axis=1)
    for c in range(cols):
        o_ref[:, c] = screened[c * rows:(c + 1) * rows].reshape(block, 2, order)

    for copies in panels + back:
        for cp, cond, _ in copies:
            when(cond, cp.wait_send)
    for k in range(count):

        def sent(k=k):
            over_y[k].wait_send()
            for b in range(2):
                over_x[k, b].wait_send()
                for a in range(2):
                    over_core[k, b, a].wait_send()

        when(held[k], sent)
        if k:
            when(line_if[k], line[k].wait_send)


def fused(n, m, lesser, greater_transposed, coulomb):
    block, _, cols, order = lesser.shape
    depth, width = coulomb.shape
    energies = n * block
    total = cols * order // LANES
    slots = -(-total // n)
    rows = 2 * block
    forward, inverse = tables(energies)
    passes = 4
    places = 1 + 2 * (n // 2 - 1)
    out = pl.pallas_call(
        functools.partial(kernel, n, m),
        out_shape=jax.ShapeDtypeStruct((block, cols, 2, order), jnp.float32),
        in_specs=[pl.BlockSpec(memory_space=pl.ANY)] * 5,
        out_specs=pl.BlockSpec(memory_space=pltpu.VMEM),
        scratch_shapes=[
            pltpu.VMEM((block, cols, 2, order), jnp.float32),
            pltpu.VMEM((block, cols, 2, order), jnp.float32),
            pltpu.VMEM((depth, width), jnp.bfloat16),
            pltpu.VMEM(forward.shape, jnp.bfloat16),
            pltpu.VMEM(inverse.shape, jnp.bfloat16),
            pltpu.VMEM((n, slots, 3 * rows, LANES), jnp.bfloat16),
            pltpu.VMEM((slots, n, 3 * rows, LANES), jnp.bfloat16),
            pltpu.VMEM((slots, n, rows, LANES), jnp.bfloat16),
            pltpu.VMEM((slots, n, rows, LANES), jnp.bfloat16),
            pltpu.VMEM((n, m, 2 * depth + depth // 3, LANES), jnp.bfloat16),
            pltpu.SemaphoreType.DMA((passes, n)),
            pltpu.SemaphoreType.DMA((passes, n)),
            pltpu.SemaphoreType.DMA((passes, n)),
            pltpu.SemaphoreType.DMA((passes, n)),
            pltpu.SemaphoreType.DMA((8 * places,)),
            pltpu.SemaphoreType.DMA((8 * places,)),
            pltpu.SemaphoreType.DMA((2,)),
            pltpu.SemaphoreType.DMA((5,)),
        ],
        compiler_params=pltpu.CompilerParams(
            collective_id=0, has_side_effects=True, vmem_limit_bytes=63 * 2**20),
        cost_estimate=pl.CostEstimate(flops=2_000_000_000, bytes_accessed=8_000_000, transcendentals=0),
    )(lesser.transpose(0, 2, 1, 3), greater_transposed.transpose(0, 2, 1, 3), coulomb,
      jnp.asarray(forward), jnp.asarray(inverse))
    return out.transpose(0, 2, 1, 3)


def solution(mesh):
    placed = (P("energy", None, "col", None), P("energy", None, "col", None), P("energy", "col"))
    n, m = mesh.shape["energy"], mesh.shape["col"]

    def local(lesser, greater_transposed, coulomb):
        depth, width = coulomb.shape
        fits = (m == 4 and n % 2 == 0 and depth % 48 == 0 and width == 2 * LANES + REST
                and lesser.shape[0] % 8 == 0 and lesser.shape[3] % LANES == 0)
        if fits:
            return fused(n, m, lesser, greater_transposed, coulomb)
        return per_device(lesser, greater_transposed, coulomb)

    return jax.shard_map(
        local,
        mesh=mesh,
        in_specs=placed,
        out_specs=P("energy", None, "col", None),
        check_vma=False,
    )
```

```python
import functools
import math

import jax
import jax.numpy as jnp
import ml_dtypes
import numpy as np
from jax import lax
from jax.experimental import pallas as pl
from jax.experimental.pallas import tpu as pltpu
from jax.sharding import PartitionSpec as P

LANES = 128
REST = 32
MESH = pl.DeviceIdType.MESH


def product(left, right):
    return jnp.dot(left, right, precision=lax.Precision.HIGHEST, preferred_element_type=jnp.float32)


def per_device(lesser, greater_transposed, coulomb):
    lesser_all, greater_all = (
        lax.all_to_all(lesser, "energy", split_axis=3, concat_axis=0, tiled=True),
        lax.all_to_all(greater_transposed, "energy", split_axis=3, concat_axis=0, tiled=True),
    )
    energies = lesser_all.shape[0]
    columns_here = lesser_all.shape[2]
    rows_here = lesser_all.shape[3]
    padded = 2 * energies
    lesser_re = lesser_all[:, 0].reshape(energies, -1)
    lesser_im = lesser_all[:, 1].reshape(energies, -1)
    greater_re = greater_all[:, 0].reshape(energies, -1)
    greater_im = greater_all[:, 1].reshape(energies, -1)
    frequency = lax.broadcasted_iota(jnp.int32, (padded, energies), 0)
    position = lax.broadcasted_iota(jnp.int32, (padded, energies), 1)
    phases = frequency * position % padded
    angles = phases.astype(jnp.float32) * (2.0 * math.pi / padded)
    cos_table = jnp.cos(angles)
    sin_table = jnp.sin(angles)
    left_re = product(cos_table, lesser_re) + product(sin_table, lesser_im)
    left_im = product(cos_table, lesser_im) - product(sin_table, lesser_re)
    right_re = product(cos_table, greater_re) - product(sin_table, greater_im)
    right_im = product(cos_table, greater_im) + product(sin_table, greater_re)
    mixed_re = left_re * right_re - left_im * right_im
    mixed_im = left_re * right_im + left_im * right_re
    corr_re = (product(cos_table.T, mixed_re) - product(sin_table.T, mixed_im)) / padded
    corr_im = (product(cos_table.T, mixed_im) + product(sin_table.T, mixed_re)) / padded
    factor = 1.0 / math.sqrt(energies)
    polar_re = (corr_im * factor).reshape(energies, columns_here, rows_here)
    polar_im = (-corr_re * factor).reshape(energies, columns_here, rows_here)
    polarized = jnp.stack([polar_re, polar_im], axis=1).astype(jnp.bfloat16)
    coulomb_wide = lax.all_gather(coulomb, "col", axis=1, tiled=True)
    order = coulomb_wide.shape[1]
    returned = lax.all_to_all(polarized, "energy", split_axis=0, concat_axis=3, tiled=True)
    flattened = returned.reshape(-1, order)
    running = jnp.dot(
        flattened,
        lax.all_gather(coulomb_wide, "energy", axis=0, tiled=True),
        preferred_element_type=jnp.float32,
    )
    screened = running.reshape(returned.shape)
    return screened


def split_table(table):
    high = table.astype(ml_dtypes.bfloat16)
    low = (table - high.astype(np.float64)).astype(ml_dtypes.bfloat16)
    return np.concatenate([high, high, low], axis=1)


def tables(energies):
    padded = 2 * energies
    angle = 2.0 * math.pi / padded * (np.outer(np.arange(padded), np.arange(energies)) % padded)
    cos, sin = np.cos(angle), np.sin(angle)
    forward_re = np.stack([cos, sin], axis=2).reshape(padded, padded)
    forward_im = np.stack([-sin, cos], axis=2).reshape(padded, padded)
    forward = np.concatenate([forward_re, forward_im], axis=0)
    scale = 1.0 / (padded * math.sqrt(energies))
    corr_re = np.concatenate([cos.T, -sin.T], axis=1)
    corr_im = np.concatenate([sin.T, cos.T], axis=1)
    inverse = np.stack([corr_im, -corr_re], axis=1).reshape(padded, 2 * padded) * scale
    return split_table(forward), split_table(inverse)


def high_low(x):
    high = x.astype(jnp.bfloat16)
    return high, (x - high.astype(jnp.float32)).astype(jnp.bfloat16)


def kernel(n, m, l_hbm, r_hbm, w_hbm, tf_hbm, ti_hbm, o_ref, l_ref, r_ref, w_ref, tf_ref, ti_ref,
           give, take, polar, panel, coul, lr_send, lr_recv, p_send, p_recv, c_send, c_recv, own_sem, load_sem):
    here_e, here_c = lax.axis_index("energy"), lax.axis_index("col")
    block, cols, _, order = l_ref.shape
    tiles_k = order // LANES
    total = cols * tiles_k
    full, extra = total // n, total % n
    slots = full + (1 if extra else 0)
    rows = 2 * block
    depth, width = w_ref.shape
    wide = width - REST
    third = depth // 3
    lead = 1 if extra else 0
    groups = [(0, slots - 1), (slots - 1, slots)] if slots > 1 else [(0, 1)]

    def slot(t):
        return (0, t) if t < extra else ((t - extra) // n + lead, (t - extra) % n)


    loads = [pltpu.make_async_copy(a, b, load_sem.at[i]) for i, (a, b) in enumerate(
        [(l_hbm, l_ref), (r_hbm, r_ref), (w_hbm, w_ref), (tf_hbm, tf_ref), (ti_hbm, ti_ref)])]
    for i in (2, 0, 1, 3, 4):
        loads[i].start()

    z, y = here_e // 2, lax.rem(here_e, 2)
    x, core = here_c // 2, lax.rem(here_c, 2)
    nz = n // 2
    peer_y = z * 2 + 1 - y
    peer_x = (1 - x) * 2 + core
    peer_core = x * 2 + 1 - core

    barrier = pltpu.get_barrier_semaphore()
    for s in range(1, n):
        pl.semaphore_signal(barrier, inc=1, device_id={"energy": lax.rem(here_e + s, n)}, device_id_type=MESH)
    for peer in (peer_x, peer_core):
        pl.semaphore_signal(barrier, inc=1, device_id={"col": peer}, device_id_type=MESH)

    sign = jnp.where(lax.broadcasted_iota(jnp.int32, (rows, LANES), 0) % 2 == 0, 1.0, -1.0)

    def pack(t):
        j, d = slot(t)
        c, k = t % cols, t // cols
        lanes = slice(k * LANES, (k + 1) * LANES)
        high, low = high_low(l_ref[:, c, :, lanes].reshape(rows, LANES))
        give[d, j, 0:rows] = high
        give[d, j, rows:2 * rows] = low
        right = r_ref[:, c, :, lanes].reshape(rows, LANES) * sign
        give[d, j, 2 * rows:3 * rows] = right.astype(jnp.bfloat16)

    def exchange(source, target, send_sems, recv_sems, send_if, recv_if):
        out = []
        for i, (start, stop) in enumerate(groups):
            copies = []
            for s in range(1, n):
                dev = lax.rem(here_e + s, n)
                begin = max(start, lead)
                if stop > begin:
                    copies.append((pltpu.make_async_remote_copy(
                        src_ref=source(begin, stop - begin, dev), dst_ref=target(begin, stop - begin),
                        send_sem=send_sems.at[2 * i, s], recv_sem=recv_sems.at[2 * i, s],
                        device_id={"energy": dev}, device_id_type=MESH), None, None))
                if start < lead:
                    copies.append((pltpu.make_async_remote_copy(
                        src_ref=source(0, 1, dev), dst_ref=target(0, 1),
                        send_sem=send_sems.at[2 * i + 1, s], recv_sem=recv_sems.at[2 * i + 1, s],
                        device_id={"energy": dev}, device_id_type=MESH), send_if(s), recv_if(s)))
            out.append(copies)
        return out

    def when(cond, f):
        if cond is None:
            f()
        else:
            pl.when(cond)(f)

    panels = exchange(
        lambda a, w, dev: give.at[dev, pl.ds(a, w)], lambda a, w: take.at[pl.ds(a, w), here_e],
        lr_send, lr_recv, lambda s: lax.rem(here_e + s, n) < extra, lambda s: here_e < extra)
    back = exchange(
        lambda a, w, dev: polar.at[pl.ds(a, w), dev], lambda a, w: panel.at[pl.ds(a, w), here_e],
        p_send, p_recv, lambda s: here_e < extra, lambda s: lax.rem(here_e + n - s, n) < extra)

    places = [(0, 0)] + [(way, s) for s in range(1, nz) for way in (1, -1)]

    def share(index, e, c, dev):
        return pltpu.make_async_remote_copy(
            src_ref=coul.at[e, c], dst_ref=coul.at[e, c], send_sem=c_send.at[index],
            recv_sem=c_recv.at[index], device_id=dev, device_id_type=MESH)

    def inside(position):
        return (position >= 0) & (position < nz)

    count = len(places)
    iz, iy, ix, ic = 0, count, 2 * count, 4 * count
    held, line, line_if, over_y, over_x, over_core = {}, {}, {}, {}, {}, {}
    for k, (way, s) in enumerate(places):
        zk = lax.rem(z - way * s + nz, nz)
        held[k] = None if k == 0 else inside(z - way * s)
        owner = (zk * 2 + y, zk * 2 + 1 - y)
        over_y[k] = share(iy + k, owner[0], here_c, {"energy": peer_y})
        for b in range(2):
            over_x[k, b] = share(ix + 2 * k + b, owner[b], here_c, {"col": peer_x})
            for a in range(2):
                over_core[k, b, a] = share(
                    ic + 4 * k + 2 * b + a, owner[b], here_c if a == 0 else peer_x, {"col": peer_core})
        if k:
            before = lax.rem(z - way * (s - 1) + nz, nz)
            line[k] = share(iz + k, before * 2 + y, here_c, {"energy": lax.rem(z + way + nz, nz) * 2 + y})
            line_if[k] = inside(z - way * (s - 1)) & inside(z + way)

    loads[2].wait()
    w = w_ref[...]
    coul[here_e, here_c, 0:depth] = w[:, 0:LANES]
    coul[here_e, here_c, depth:2 * depth] = w[:, LANES:2 * LANES]
    rest = w[:, wide:].astype(jnp.float32)
    packed = jnp.concatenate(
        [rest[q * third:(q + 1) * third] for q in range(3)] + [jnp.zeros((third, LANES - 3 * REST), jnp.float32)],
        axis=1)
    coul[here_e, here_c, 2 * depth:2 * depth + third] = packed.astype(jnp.bfloat16)
    pl.semaphore_wait(barrier, n - 1 + 2)
    for k, (way, s) in enumerate(places):
        if s == 1:
            when(line_if[k], line[k].start)
    over_y[0].start()
    over_x[0, 0].start()
    over_core[0, 0, 0].start()

    loads[0].wait()
    loads[1].wait()
    first = extra + (groups[0][1] - lead) * n
    for t in range(first):
        pack(t)
    for cp, cond, _ in panels[0]:
        when(cond, cp.start)

    for t in range(first, total):
        pack(t)
    for copies in panels[1:]:
        for cp, cond, _ in copies:
            when(cond, cp.start)
    own = pltpu.make_async_copy(give.at[here_e], take.at[:, here_e], own_sem.at[0])
    own.start()

    def relay_z(distance):
        for k, (way, s) in enumerate(places):
            if s != distance:
                continue

            def pass_on(k=k, s=s, way=way):
                line[k].wait_recv()
                if s + 1 < nz:
                    after = places.index((way, s + 1))
                    pl.when(line_if[after])(line[after].start)
                over_y[k].start()
                over_x[k, 0].start()
                over_core[k, 0, 0].start()

            when(held[k], pass_on)

    def relay_y(distance):
        for k, (way, s) in enumerate(places):
            if s != distance:
                continue

            def pass_y(k=k):
                over_y[k].wait_recv()
                over_x[k, 1].start()
                over_core[k, 1, 0].start()

            when(held[k], pass_y)

    def relay_x(distance):
        for k, (way, s) in enumerate(places):
            if s != distance:
                continue

            def pass_x(k=k):
                for b in range(2):
                    over_x[k, b].wait_recv()
                    over_core[k, b, 1].start()

            when(held[k], pass_x)

    span = n * rows

    def correlate(i):
        start, stop = groups[i]
        for cp, _, cond in panels[i]:
            when(cond, cp.wait_recv)

        def piece(p):
            return jnp.concatenate(
                [take[j, :, p * rows:(p + 1) * rows].reshape(span, LANES) for j in range(start, stop)], axis=1)

        l_high, l_low, r_high = piece(0), piece(1), piece(2)
        left = jnp.dot(tf_ref[...], jnp.concatenate([l_high, l_low, l_high], axis=0),
                       preferred_element_type=jnp.float32)
        right = jnp.dot(tf_ref[:, span:], jnp.concatenate([r_high, r_high], axis=0),
                        preferred_element_type=jnp.float32)
        a, b = left[:span], left[span:]
        c, d = right[:span], right[span:]
        mixed = jnp.concatenate([a * c + b * d, b * c - a * d], axis=0)
        m_high, m_low = high_low(mixed)
        polarized = jnp.dot(ti_ref[...], jnp.concatenate([m_high, m_low, m_high], axis=0),
                            preferred_element_type=jnp.float32).astype(jnp.bfloat16)
        for j in range(start, stop):
            polar[j] = polarized[:, (j - start) * LANES:(j - start + 1) * LANES].reshape(n, rows, LANES)
        for cp, cond, _ in back[i]:
            when(cond, cp.start)

    relay_z(1)
    relay_y(0)
    for s in range(2, nz - 1):
        relay_z(s)
        relay_y(s - 1)
    if nz > 2:
        relay_z(nz - 1)
        relay_y(nz - 2)
    relay_y(nz - 1)
    loads[3].wait()
    loads[4].wait()
    own.wait()
    correlate(0)
    for s in range(min(2, nz)):
        relay_x(s)
    for i in range(1, len(groups)):
        correlate(i)
    own_p = pltpu.make_async_copy(polar.at[:, here_e], panel.at[:, here_e], own_sem.at[1])
    own_p.start()

    for s in range(2, nz):
        relay_x(s)
    for k in range(count):

        def arrive(k=k):
            for b in range(2):
                for a in range(2):
                    over_core[k, b, a].wait_recv()

        when(held[k], arrive)

    lane = lax.broadcasted_iota(jnp.int32, (third, LANES), 1)
    rests = []
    for g in range(n):
        for q in range(3):
            acc = jnp.zeros((third, LANES), jnp.float32)
            for cc in range(m):
                u = coul[g, cc, 2 * depth:2 * depth + third].astype(jnp.float32)
                shift = (cc - q) * REST % LANES
                if shift:
                    u = pltpu.roll(u, shift, 1)
                acc = jnp.where((lane >= cc * REST) & (lane < (cc + 1) * REST), u, acc)
            rests.append(acc.astype(jnp.bfloat16))
    rest_all = jnp.concatenate(rests, axis=0)

    def multiply(low, high):
        flat = jnp.concatenate(
            [jnp.concatenate([panel[slot(k * cols + c)] for k in range(low, high)], axis=1) for c in range(cols)],
            axis=0)
        part = slice(low * LANES, high * LANES)
        out = []
        for cc in range(m):
            weight = jnp.concatenate(
                [coul[:, cc, h * depth:(h + 1) * depth].reshape(n * depth, LANES)[part] for h in range(2)], axis=1)
            out.append(jnp.dot(flat, weight, preferred_element_type=jnp.float32))
        out.append(jnp.dot(flat, rest_all[part], preferred_element_type=jnp.float32))
        return out

    own_p.wait()
    cut = first // cols
    sums = None
    for i, copies in enumerate(back):
        for cp, _, cond in copies:
            when(cond, cp.wait_recv)
        low, high = (0 if i == 0 else cut), (tiles_k if i == len(back) - 1 else cut)
        if high > low:
            terms = multiply(low, high)
            sums = terms if sums is None else [p + q for p, q in zip(sums, terms)]
    pieces = []
    for cc in range(m):
        pieces.append(sums[cc])
        pieces.append(sums[m][:, cc * REST:(cc + 1) * REST])
    screened = jnp.concatenate(pieces, axis=1)
    for c in range(cols):
        o_ref[:, c] = screened[c * rows:(c + 1) * rows].reshape(block, 2, order)

    for copies in panels + back:
        for cp, cond, _ in copies:
            when(cond, cp.wait_send)
    for k in range(count):

        def sent(k=k):
            over_y[k].wait_send()
            for b in range(2):
                over_x[k, b].wait_send()
                for a in range(2):
                    over_core[k, b, a].wait_send()

        when(held[k], sent)
        if k:
            when(line_if[k], line[k].wait_send)


def fused(n, m, lesser, greater_transposed, coulomb):
    block, _, cols, order = lesser.shape
    depth, width = coulomb.shape
    energies = n * block
    total = cols * order // LANES
    slots = -(-total // n)
    rows = 2 * block
    forward, inverse = tables(energies)
    passes = 4
    places = 1 + 2 * (n // 2 - 1)
    out = pl.pallas_call(
        functools.partial(kernel, n, m),
        out_shape=jax.ShapeDtypeStruct((block, cols, 2, order), jnp.float32),
        in_specs=[pl.BlockSpec(memory_space=pl.ANY)] * 5,
        out_specs=pl.BlockSpec(memory_space=pltpu.VMEM),
        scratch_shapes=[
            pltpu.VMEM((block, cols, 2, order), jnp.float32),
            pltpu.VMEM((block, cols, 2, order), jnp.float32),
            pltpu.VMEM((depth, width), jnp.bfloat16),
            pltpu.VMEM(forward.shape, jnp.bfloat16),
            pltpu.VMEM(inverse.shape, jnp.bfloat16),
            pltpu.VMEM((n, slots, 3 * rows, LANES), jnp.bfloat16),
            pltpu.VMEM((slots, n, 3 * rows, LANES), jnp.bfloat16),
            pltpu.VMEM((slots, n, rows, LANES), jnp.bfloat16),
            pltpu.VMEM((slots, n, rows, LANES), jnp.bfloat16),
            pltpu.VMEM((n, m, 2 * depth + depth // 3, LANES), jnp.bfloat16),
            pltpu.SemaphoreType.DMA((passes, n)),
            pltpu.SemaphoreType.DMA((passes, n)),
            pltpu.SemaphoreType.DMA((passes, n)),
            pltpu.SemaphoreType.DMA((passes, n)),
            pltpu.SemaphoreType.DMA((8 * places,)),
            pltpu.SemaphoreType.DMA((8 * places,)),
            pltpu.SemaphoreType.DMA((2,)),
            pltpu.SemaphoreType.DMA((5,)),
        ],
        compiler_params=pltpu.CompilerParams(
            collective_id=0, has_side_effects=True, vmem_limit_bytes=63 * 2**20),
        cost_estimate=pl.CostEstimate(flops=2_000_000_000, bytes_accessed=8_000_000, transcendentals=0),
    )(lesser.transpose(0, 2, 1, 3), greater_transposed.transpose(0, 2, 1, 3), coulomb,
      jnp.asarray(forward), jnp.asarray(inverse))
    return out.transpose(0, 2, 1, 3)


def solution(mesh):
    placed = (P("energy", None, "col", None), P("energy", None, "col", None), P("energy", "col"))
    n, m = mesh.shape["energy"], mesh.shape["col"]

    def local(lesser, greater_transposed, coulomb):
        depth, width = coulomb.shape
        fits = (m == 4 and n % 2 == 0 and depth % 48 == 0 and width == 2 * LANES + REST
                and lesser.shape[0] % 8 == 0 and lesser.shape[3] % LANES == 0)
        if fits:
            return fused(n, m, lesser, greater_transposed, coulomb)
        return per_device(lesser, greater_transposed, coulomb)

    return jax.shard_map(
        local,
        mesh=mesh,
        in_specs=placed,
        out_specs=P("energy", None, "col", None),
        check_vma=False,
    )
```
